1024 devices in a mesh: ctx: 16 (over z), head: 64 (over x, y, core).
Axes of the slice: x: 4, y: 8, z: 16, core: 2. Of those that a mesh axis runs over, the one named last changes fastest.
Arguments:
- queries: bfloat16 [32768, 64, 128], P('ctx', 'head'), may hold values from -54 to 54
- keys: bfloat16 [32768, 8, 128], P(('ctx', 'head')), may hold values from -12 to 12
- values: bfloat16 [32768, 8, 128], P(('ctx', 'head')), may hold values from -6 to 6
- key_blocks: int32 [256, 4], replicated, may hold values from 0 to 255, as said below
- span_order: int32 [32], replicated, may hold values from 0 to 31, as said below
Outputs:
- attended: bfloat16 [32768, 64, 128], P('ctx', 'head')
The draws below stay inside these ranges and needn't reach their ends.
Inputs may be any that keep to these rules, and one draw needn't show every extreme that they name: `key_blocks`: row b names block b in slot 0; each used slot j (1 <= j <= b) names a block below b, and a block may stand in two slots of a row; unused slots hold 0. The query blocks of one ctx index list at most 2 distinct blocks held by any one other ctx index. `span_order`: each number once.
All inputs are finite; a program needn't handle non-finite values.
Results may differ from the reference program's by a relative error of at most 0.0045.
Values may be sent and summed in bfloat16 or wider, within the bound.
No kernel may reach another device: no remote copies, remote signals or barrier semaphores. Data moves between devices by JAX's collectives and lax.ppermute only.
A program may use at most 32 MiB of HBM per device.

```python
import jax
import jax.numpy as jnp
from jax import lax

H = 64
KVH = 8
DH = 128
BLK = 128
KB = 4
CAP = 2
S_DEV = 2048
SEQ = 32768
NB = 256
N_CTX = 16


def shared_pair(key):
    seeded = jax.random.fold_in(key, 7)
    key_drawn = jnp.clip(jax.random.normal(jax.random.fold_in(seeded, 1), (SEQ, KVH, DH), jnp.float32), -4.0, 4.0)
    query_drawn = jnp.clip(jax.random.normal(jax.random.fold_in(seeded, 4), (SEQ, H, DH), jnp.float32), -4.0, 4.0)
    key_values = key_drawn
    query_values = query_drawn
    return (query_values, key_values)


def draw_queries(key, part):
    return shared_pair(key)[0].astype(jnp.bfloat16)


def draw_keys(key, part):
    return shared_pair(key)[1].astype(jnp.bfloat16)


def span_layout(key):
    seeded = jax.random.fold_in(key, 31)
    span_total = 2 * N_CTX
    priority = jax.random.randint(seeded, (span_total,), 0, 1 << 12) * span_total + jnp.arange(span_total, dtype=jnp.int32)
    return jnp.argsort(priority).astype(jnp.int32)


def draw_span_order(key, part):
    return span_layout(key)


def draw_key_blocks(key, part):
    layout = span_layout(key)
    per_span = S_DEV // (2 * BLK)
    block_count = S_DEV // BLK
    span_ids = jnp.arange(2 * N_CTX, dtype=jnp.int32)
    inverse = jnp.sum(jnp.where(layout[None, :] == span_ids[:, None], span_ids[None, :], 0), axis=1).astype(jnp.int32)
    block_ids = jnp.arange(NB, dtype=jnp.int32)
    holder = inverse[block_ids // per_span] // 2
    device_ids = jnp.arange(N_CTX, dtype=jnp.int32)
    local_ids = jnp.arange(block_count, dtype=jnp.int32)
    held = layout[2 * device_ids[:, None] + local_ids[None, :] // per_span] * per_span + local_ids[None, :] % per_span
    priority = jax.random.randint(jax.random.fold_in(key, 41), (N_CTX, N_CTX, block_count), 0, 1 << 12) * block_count + local_ids[None, None, :]
    priority = priority - jnp.where(held[None, :, :] < 2, 1 << 22, 0)
    chosen = jnp.argsort(priority, axis=2)[:, :, :CAP].astype(jnp.int32)
    set_pos = jnp.take_along_axis(jnp.broadcast_to(held[None, :, :], (N_CTX, N_CTX, block_count)), chosen, axis=2)
    member = jnp.any(jnp.take(set_pos, holder, axis=1) == block_ids[None, :, None], axis=2)
    member_rows = jnp.take(member, holder, axis=0)
    candidate = (block_ids[None, :] < block_ids[:, None]) & ((holder[None, :] == holder[:, None]) | member_rows)
    available = jnp.sum(candidate.astype(jnp.int32), axis=1)
    nonzero = jnp.maximum(available, 1)
    running = jnp.cumsum(candidate.astype(jnp.int32), axis=1)
    offset = jax.random.randint(jax.random.fold_in(key, 42), (NB,), 0, 1 << 12)
    picked = [block_ids]
    for slot_index in range(1, KB):
        target = (offset + slot_index - 1) % nonzero
        picked.append(jnp.sum((running <= target[:, None]).astype(jnp.int32), axis=1).astype(jnp.int32))
    listed = jnp.stack(picked, axis=1)
    last_holder = holder[NB - 1]
    other_holder = (last_holder + 1) % N_CTX
    forced = set_pos[last_holder, other_holder]
    listed = listed.at[NB - 1, 1:1 + CAP].set(forced)
    in_use = jnp.arange(KB, dtype=jnp.int32)[None, :] <= block_ids[:, None]
    return jnp.where(in_use, listed, 0).astype(jnp.int32)


def level_of(own_key, dims, cuts, least, high):
    loudness, own = 1.0, jax.random.fold_in(own_key, 6)
    for axis_at, blocks in cuts:
        draws = jnp.exp(jax.random.uniform(jax.random.fold_in(own, axis_at), (blocks,), jnp.float32, least / len(cuts), high / len(cuts)))
        loudness = loudness * jnp.repeat(draws, dims[axis_at] // blocks).reshape([-1 if axis == axis_at else 1 for axis in range(len(dims))])
    return loudness


def normal_values(stream_key, shape, width, most, cuts=(), kind=jnp.bfloat16):
    values = width * jax.random.normal(stream_key, shape, jnp.float32)
    if cuts:
        values = values * level_of(stream_key, shape, cuts, -0.22, 0.18)
    return jnp.clip(values, -most, most).astype(kind)


def setup_inputs(seed: int = 0) -> dict:
    arg_keys = jax.random.split(jax.random.key(seed), 6)
    return {
        "queries": draw_queries(jax.random.fold_in(arg_keys[5], 71), 0),
        "keys": draw_keys(jax.random.fold_in(arg_keys[5], 71), 0),
        "values": normal_values(arg_keys[2], (SEQ, KVH, DH), 1.0, 6.0, ((0, 1024),)),
        "key_blocks": draw_key_blocks(jax.random.fold_in(arg_keys[5], 71), 0),
        "span_order": draw_span_order(jax.random.fold_in(arg_keys[5], 71), 0),
    }


def reference(queries, keys, values, key_blocks, span_order):
    span_rows = S_DEV // 2
    slot_ids = jnp.arange(2 * N_CTX, dtype=jnp.int32)
    inverse = jnp.sum(jnp.where(span_order[None, :] == slot_ids[:, None], slot_ids[None, :], 0), axis=1).astype(jnp.int32)
    group_size = H // KVH
    score_scale = DH ** -0.5
    causal = jnp.arange(BLK)[None, :] <= jnp.arange(BLK)[:, None]

    def one_block(block_index):
        first_row = block_index * BLK
        position_block = span_order[first_row // span_rows] * (span_rows // BLK) + (first_row % span_rows) // BLK
        query_tile = lax.dynamic_slice_in_dim(queries, first_row, BLK, 0).astype(jnp.float32).reshape(BLK, KVH, group_size, DH)
        listed = key_blocks[position_block]
        in_use = jnp.arange(KB) <= position_block
        key_first = (inverse[(listed * BLK) // span_rows] * span_rows + (listed * BLK) % span_rows).astype(jnp.int32)
        key_tiles = jnp.stack([lax.dynamic_slice_in_dim(keys, key_first[slot_index], BLK, 0) for slot_index in range(KB)]).astype(jnp.float32)
        value_tiles = jnp.stack([lax.dynamic_slice_in_dim(values, key_first[slot_index], BLK, 0) for slot_index in range(KB)]).astype(jnp.float32)
        scores = jnp.einsum('qagd,jkad->agqjk', query_tile, key_tiles, precision=lax.Precision.HIGHEST) * score_scale
        allowed = in_use[None, :, None] & ((listed != position_block)[None, :, None] | causal[:, None, :])
        scores = jnp.where(allowed, scores, jnp.float32(-1e30))
        row_peak = jnp.max(scores, axis=(3, 4), keepdims=True)
        raised = jnp.exp(scores - row_peak)
        row_total = jnp.sum(raised, axis=(3, 4))
        weights = raised.astype(jnp.bfloat16).astype(jnp.float32)
        combined = jnp.einsum('agqjk,jkad->qagd', weights, value_tiles, precision=lax.Precision.HIGHEST)
        result = combined / jnp.transpose(row_total, (2, 0, 1))[..., None]
        return result.reshape(BLK, H, DH).astype(jnp.bfloat16)

    blocks_out = lax.map(one_block, jnp.arange(SEQ // BLK, dtype=jnp.int32))
    return blocks_out.reshape(SEQ, H, DH)
```

```python
import jax
import jax.numpy as jnp
from jax import lax
from jax.experimental import pallas as pl
from jax.experimental.pallas import tpu as pltpu
from jax.sharding import PartitionSpec as P

BLK = 128
CAP = 2
LOG2E = 1.4426950408889634


def pick_first(index_ref, table_ref, out_ref):
    for i in range(out_ref.shape[0]):
        out_ref[i] = table_ref[index_ref[i]]


def pick_second(index_ref, own_ref, foreign_ref, out_ref):
    own_count = own_ref.shape[0]
    for i in range(out_ref.shape[0]):
        at = index_ref[i]
        mine = own_ref[jnp.minimum(at, own_count - 1)]
        theirs = foreign_ref[jnp.maximum(at - own_count, 0)]
        out_ref[i] = jnp.where(at < own_count, mine, theirs)


def attend(pos_ref, query_ref, pair_ref, out_ref, key_all, value_all):
    pieces, pair_count, _, rows, width = pair_ref.shape
    heads = query_ref.shape[0]
    blocks = query_ref.shape[1] // BLK
    slots = pair_count // blocks
    factor = (width ** -0.5) * LOG2E
    row = lax.broadcasted_iota(jnp.int32, (BLK, BLK), 0)
    col = lax.broadcasted_iota(jnp.int32, (BLK, BLK), 1)
    piece = col // rows
    half = pieces // 2
    key_row = 2 * rows * (piece % half) + rows * (piece // half) + col % rows
    causal = key_row <= row
    for b in range(blocks):
        for j in range(slots):
            i = b * slots + j
            key_all[b, pl.ds(j * BLK, BLK), :] = pair_ref[:, i, 0].reshape(BLK, width)
            value_all[b, pl.ds(j * BLK, BLK), :] = pair_ref[:, i, 1].reshape(BLK, width)
    for b in range(blocks):
        pos = pos_ref[b]

        def one_head(h, carry):
            q = query_ref[h, pl.ds(b * BLK, BLK), :]
            s = lax.dot_general(
                q, key_all[b], (((1,), (1,)), ((), ())), preferred_element_type=jnp.float32
            )
            parts = [jnp.where(causal, s[:, :BLK], -1e30)]
            for j in range(1, slots):
                parts.append(jnp.where(pos >= j, s[:, j * BLK:(j + 1) * BLK], -1e30))
            s = jnp.concatenate(parts, axis=1)
            peak = jnp.max(s, axis=1, keepdims=True)
            raised = jnp.exp2((s - peak) * factor)
            total = jnp.sum(raised, axis=1, keepdims=True)
            mixed = jnp.dot(
                raised.astype(jnp.bfloat16), value_all[b], preferred_element_type=jnp.float32
            )
            out_ref[h, pl.ds(b * BLK, BLK), :] = (mixed / total).astype(jnp.bfloat16)
            return carry

        lax.fori_loop(0, heads, one_head, 0, unroll=2)


def body(queries, keys, values, key_blocks, span_order):
    ctx_count = lax.axis_size("ctx")
    head_count = lax.axis_size("head")
    rows_device, _, width = queries.shape
    shard_rows, kv_heads, _ = keys.shape
    slot_count = key_blocks.shape[1]
    block_count = rows_device // BLK
    per_span = block_count // 2
    group = head_count // kv_heads
    shards_per_block = BLK // shard_rows
    halves = group // shards_per_block
    piece_rows = shard_rows // halves
    me = lax.axis_index("ctx")
    rank = lax.axis_index("head") % group
    i32 = jnp.int32

    spread_groups = [
        [shards_per_block * j + q for j in range(block_count)] for q in range(shards_per_block)
    ]
    kv = jnp.stack([keys, values])
    kv = kv.reshape(2, halves, piece_rows, kv_heads, width).transpose(3, 1, 0, 2, 4)
    kv = kv.reshape(block_count, 2, piece_rows, width)
    own = lax.all_to_all(kv, "head", 0, 0, tiled=True, axis_index_groups=spread_groups)

    span_ids = jnp.arange(2 * ctx_count, dtype=i32)
    by_span = key_blocks.reshape(2 * ctx_count, per_span * slot_count)
    stored = jnp.take(by_span, span_order, axis=0)
    lane = jnp.arange(per_span * slot_count, dtype=i32)[None, :]
    position = span_order[:, None] * per_span + lane // slot_count
    in_use = lane % slot_count <= position
    my_spans = lax.dynamic_slice(span_order, (2 * me,), (2,))
    listed_span = stored // per_span
    second = listed_span == my_spans[1]
    from_me = in_use & (second | (listed_span == my_spans[0]))
    local_block = stored % per_span + jnp.where(second, per_span, 0)
    lowest = jnp.where(from_me, local_block, block_count - 1).reshape(ctx_count, -1).min(axis=1)
    highest = jnp.where(from_me, local_block, 0).reshape(ctx_count, -1).max(axis=1)
    chosen = jnp.stack([lowest, highest], axis=1).reshape(-1)

    mine = lax.dynamic_slice(stored, (2 * me, 0), (2, per_span * slot_count)).reshape(-1)
    mine_used = lax.dynamic_slice(in_use, (2 * me, 0), (2, per_span * slot_count)).reshape(-1)
    stored_at = jnp.sum(
        jnp.where(span_order[None, :] == (mine // per_span)[:, None], span_ids[None, :], 0), axis=1
    )
    owner = stored_at // 2
    held = stored_at % 2 * per_span + mine % per_span
    lower = mine_used[None, :] & (owner[None, :] == owner[:, None]) & (held[None, :] < held[:, None])
    upper = jnp.any(lower, axis=1).astype(i32)
    source = jnp.where(owner == me, held, block_count + owner * CAP + upper)
    local_ids = jnp.arange(block_count, dtype=i32)
    own_pos = my_spans[local_ids // per_span] * per_span + local_ids % per_span
    per_rank = block_count // group
    query_pos = lax.dynamic_slice(own_pos, (rank * per_rank,), (per_rank,))

    smem = pl.BlockSpec(memory_space=pltpu.SMEM)
    vmem = pl.BlockSpec(memory_space=pltpu.VMEM)
    piece = (2, piece_rows, width)

    asked = pl.pallas_call(
        pick_first,
        out_shape=jax.ShapeDtypeStruct((ctx_count * CAP,) + piece, jnp.bfloat16),
        in_specs=[smem, vmem],
        out_specs=vmem,
    )(chosen, own)
    foreign = lax.all_to_all(asked, "ctx", 0, 0, tiled=True)

    kv_groups = [[g * group + i for i in range(group)] for g in range(kv_heads)]
    query_rows = queries.reshape(group, rows_device // group, width)
    query_rows, own_after = lax.optimization_barrier((query_rows, own))
    query_here = lax.all_to_all(
        query_rows, "head", 0, 0, tiled=True, axis_index_groups=kv_groups
    )
    pairs = pl.pallas_call(
        pick_second,
        out_shape=jax.ShapeDtypeStruct((block_count * slot_count,) + piece, jnp.bfloat16),
        in_specs=[smem, vmem, vmem],
        out_specs=vmem,
    )(source, own_after, foreign)
    pairs = lax.all_to_all(pairs, "head", 0, 0, tiled=True, axis_index_groups=kv_groups)
    pairs = pairs.reshape((group, per_rank * slot_count) + piece)

    done = pl.pallas_call(
        attend,
        out_shape=jax.ShapeDtypeStruct(query_here.shape, jnp.bfloat16),
        in_specs=[smem, vmem, vmem],
        out_specs=vmem,
        scratch_shapes=[pltpu.VMEM((per_rank, slot_count * BLK, width), jnp.bfloat16)] * 2,
        compiler_params=pltpu.CompilerParams(vmem_limit_bytes=24 * 2**20),
    )(query_pos, query_here, pairs)

    out = lax.all_to_all(done, "head", 0, 0, tiled=True, axis_index_groups=kv_groups)
    return out.reshape(rows_device, 1, width)


def solution(mesh):
    in_specs = (
        P("ctx", "head", None),
        P(("ctx", "head"), None, None),
        P(("ctx", "head"), None, None),
        P(),
        P(),
    )
    out_specs = P("ctx", "head", None)
    return jax.shard_map(body, mesh=mesh, in_specs=in_specs, out_specs=out_specs, check_vma=False)
```

```python
import functools

import jax
import jax.numpy as jnp
from jax import lax
from jax.experimental import pallas as pl
from jax.experimental.pallas import tpu as pltpu
from jax.sharding import PartitionSpec as P

BLK = 128
CAP = 2
LOG2E = 1.4426950408889634
MASKED = -1e30
SMEM = pl.BlockSpec(memory_space=pltpu.SMEM)
VMEM = pl.BlockSpec(memory_space=pltpu.VMEM)


def small(mib=4):
    return pltpu.CompilerParams(vmem_limit_bytes=mib * 2**20)


def asked_range(per_span, me_ref, span_ref, listed_ref, out_ref):
    listed = listed_ref[...]
    slots, positions = listed.shape
    first = span_ref[2 * me_ref[0]]
    second = span_ref[2 * me_ref[0] + 1]
    slot = lax.broadcasted_iota(jnp.int32, listed.shape, 0)
    position = lax.broadcasted_iota(jnp.int32, listed.shape, 1)
    span = listed // per_span
    mine = (slot <= position) & ((span == first) | (span == second))
    block = listed % per_span + jnp.where(span == second, per_span, 0)
    low = jnp.min(jnp.where(mine, block, 2 * per_span - 1), axis=0, keepdims=True)
    high = jnp.max(jnp.where(mine, block, 0), axis=0, keepdims=True)
    low = jnp.broadcast_to(low, (8, positions))
    high = jnp.broadcast_to(high, (8, positions))
    step = 1
    while step < per_span:
        low = jnp.minimum(low, pltpu.roll(low, positions - step, 1))
        high = jnp.maximum(high, pltpu.roll(high, positions - step, 1))
        step *= 2
    out_ref[0:1, :] = low[0:1]
    out_ref[1:2, :] = high[0:1]


def pick_asked(per_span, span_ref, range_ref, own_ref, out_ref):
    for d in range(out_ref.shape[0] // CAP):
        a = span_ref[2 * d] * per_span
        b = span_ref[2 * d + 1] * per_span
        out_ref[2 * d] = own_ref[jnp.minimum(range_ref[0, a], range_ref[0, b])]
        out_ref[2 * d + 1] = own_ref[jnp.maximum(range_ref[1, a], range_ref[1, b])]


def find_sources(per_span, me_ref, span_ref, listed_ref, out_ref, inverse, lowest, owners, helds):
    me = me_ref[0]
    slots = listed_ref.shape[0]
    span_count = span_ref.shape[0]
    blocks = 2 * per_span

    def invert(s, carry):
        inverse[span_ref[s]] = s
        return carry

    def reset(s, carry):
        lowest[s] = blocks
        return carry

    lax.fori_loop(0, span_count, invert, 0, unroll=4)
    lax.fori_loop(0, span_count // 2, reset, 0, unroll=4)

    def scan(block, carry):
        position = span_ref[2 * me + block // per_span] * per_span + block % per_span
        for j in range(1, slots):
            name = listed_ref[j, position]
            at = inverse[name // per_span]
            owner = at // 2
            held = at % 2 * per_span + name % per_span
            owners[block * slots + j] = owner
            helds[block * slots + j] = held
            lowest[owner] = jnp.minimum(lowest[owner], jnp.where(j <= position, held, blocks))
        return carry

    lax.fori_loop(0, blocks, scan, 0, unroll=2)

    def place(block, carry):
        out_ref[block * slots] = block
        for j in range(1, slots):
            owner = owners[block * slots + j]
            held = helds[block * slots + j]
            foreign = blocks + CAP * owner + jnp.where(held > lowest[owner], 1, 0)
            out_ref[block * slots + j] = jnp.where(owner == me, held, foreign)
        return carry

    lax.fori_loop(0, blocks, place, 0, unroll=2)


def pick_pairs(source_ref, own_ref, foreign_ref, out_ref):
    own_count = own_ref.shape[0]
    for i in range(out_ref.shape[0]):
        at = source_ref[i]
        mine = own_ref[jnp.minimum(at, own_count - 1)]
        theirs = foreign_ref[jnp.maximum(at - own_count, 0)]
        out_ref[i] = jnp.where(at < own_count, mine, theirs)


def bundle(rank_ref, query_ref, sibling_ref, *out_refs):
    chip = rank_ref[0] // 2
    core = rank_ref[0] % 2
    for k, out_ref in enumerate(out_refs):
        to = chip ^ k
        out_ref[0] = query_ref[2 * to + core]
        out_ref[1] = sibling_ref[to]


def attend(per_span, me_ref, rank_ref, span_ref, *refs):
    *query_refs, pair_ref, out_ref, key_all, value_all = refs
    pieces, pair_count, _, rows, width = pair_ref.shape
    blocks = key_all.shape[0]
    slots = pair_count // blocks
    factor = (width ** -0.5) * LOG2E
    chip = rank_ref[0] // 2
    core = rank_ref[0] % 2
    row = lax.broadcasted_iota(jnp.int32, (BLK, BLK), 0)
    col = lax.broadcasted_iota(jnp.int32, (BLK, BLK), 1)
    piece = col // rows
    half = pieces // 2
    causal = 2 * rows * (piece % half) + rows * (piece // half) + col % rows <= row
    causal = jnp.concatenate([causal, causal], axis=0)
    for b in range(blocks):
        for j in range(slots):
            i = b * slots + j
            key_all[b, j * BLK:(j + 1) * BLK, :] = pair_ref[:, i, 0].reshape(BLK, width)
            value_all[b, j * BLK:(j + 1) * BLK, :] = pair_ref[:, i, 1].reshape(BLK, width)
    for b in range(blocks):
        block = rank_ref[0] * blocks + b
        position = span_ref[2 * me_ref[0] + block // per_span] * per_span + block % per_span
        here = slice(b * BLK, (b + 1) * BLK)
        for k, query_ref in enumerate(query_refs):
            q = query_ref[:, here, :].reshape(2 * BLK, width)
            s = lax.dot_general(
                q, key_all[b], (((1,), (1,)), ((), ())), preferred_element_type=jnp.float32
            )
            parts = [jnp.where(causal, s[:, :BLK], MASKED)]
            for j in range(1, slots):
                parts.append(jnp.where(position >= j, s[:, j * BLK:(j + 1) * BLK], MASKED))
            peak = functools.reduce(jnp.maximum, parts)
            peak = jnp.max(peak, axis=1, keepdims=True) * factor
            total = jnp.zeros((2 * BLK, BLK), jnp.float32)
            mixed = jnp.zeros((2 * BLK, width), jnp.float32)
            for j in range(slots):
                raised = jnp.exp2(parts[j] * factor - peak)
                total += raised
                mixed += jnp.dot(
                    raised.astype(jnp.bfloat16),
                    value_all[b, j * BLK:(j + 1) * BLK],
                    preferred_element_type=jnp.float32,
                )
            total = jnp.sum(total, axis=1, keepdims=True)
            result = (mixed * (1.0 / total)).astype(jnp.bfloat16)
            out_ref[2 * (chip ^ k) + core, here, :] = result[:BLK]
            out_ref[2 * (chip ^ k) + 1 - core, here, :] = result[BLK:]


def body(queries, keys, values, key_blocks, span_order):
    ctx_count = lax.axis_size("ctx")
    head_count = lax.axis_size("head")
    rows_device, _, width = queries.shape
    shard_rows, kv_heads, _ = keys.shape
    slot_count = key_blocks.shape[1]
    block_count = rows_device // BLK
    per_span = block_count // 2
    group = head_count // kv_heads
    shards_per_block = BLK // shard_rows
    halves = group // shards_per_block
    piece_rows = shard_rows // halves
    per_rank = block_count // group
    chips = group // 2
    i32 = jnp.int32
    bf16 = jnp.bfloat16
    me = lax.axis_index("ctx").astype(i32)
    rank = lax.rem(lax.axis_index("head").astype(i32), group)
    piece = (2, piece_rows, width)
    listed = key_blocks.T

    spread_groups = [
        [shards_per_block * j + q for j in range(block_count)] for q in range(shards_per_block)
    ]
    kv = jnp.stack([keys, values])
    kv = kv.reshape(2, halves, piece_rows, kv_heads, width).transpose(3, 1, 0, 2, 4)
    kv = kv.reshape((block_count,) + piece)
    own = lax.all_to_all(kv, "head", 0, 0, tiled=True, axis_index_groups=spread_groups)

    ranges = pl.pallas_call(
        functools.partial(asked_range, per_span),
        out_shape=jax.ShapeDtypeStruct((2, key_blocks.shape[0]), i32),
        in_specs=[SMEM, SMEM, VMEM],
        out_specs=VMEM,
        compiler_params=small(),
    )(me[None], span_order, listed)

    asked = pl.pallas_call(
        functools.partial(pick_asked, per_span),
        out_shape=jax.ShapeDtypeStruct((ctx_count * CAP,) + piece, bf16),
        in_specs=[SMEM, SMEM, VMEM],
        out_specs=VMEM,
        compiler_params=small(),
    )(span_order, ranges, own)
    foreign = lax.all_to_all(asked, "ctx", 0, 0, tiled=True)

    core = lax.rem(rank, 2)
    query_parts = queries.reshape(chips, 2, rows_device // group, width)
    query_parts, span_after, _ = lax.optimization_barrier((query_parts, span_order, asked))
    crossing = lax.dynamic_index_in_dim(query_parts, 1 - core, 1, keepdims=False)
    sibling = lax.ppermute(crossing, "head", [(i, i ^ 1) for i in range(head_count)])
    part = jax.ShapeDtypeStruct((2, rows_device // group, width), bf16)
    bundles = pl.pallas_call(
        bundle,
        out_shape=(part,) * chips,
        in_specs=[SMEM, VMEM, VMEM],
        out_specs=(VMEM,) * chips,
        compiler_params=small(8),
    )(rank[None], query_parts.reshape(group, rows_device // group, width), sibling)
    source = pl.pallas_call(
        functools.partial(find_sources, per_span),
        out_shape=jax.ShapeDtypeStruct((block_count * slot_count,), i32),
        in_specs=[SMEM, SMEM, SMEM],
        out_specs=SMEM,
        scratch_shapes=[
            pltpu.SMEM((2 * ctx_count,), i32),
            pltpu.SMEM((ctx_count,), i32),
            pltpu.SMEM((block_count * slot_count,), i32),
            pltpu.SMEM((block_count * slot_count,), i32),
        ],
        compiler_params=small(),
    )(me[None], span_after, listed)
    query_here = [bundles[0]] + [
        lax.ppermute(bundles[k], "head", [(i, i ^ (2 * k)) for i in range(head_count)])
        for k in range(1, chips)
    ]
    source, _ = lax.optimization_barrier((source, bundles))

    kv_groups = [[g * group + i for i in range(group)] for g in range(kv_heads)]
    pairs = pl.pallas_call(
        pick_pairs,
        out_shape=jax.ShapeDtypeStruct((block_count * slot_count,) + piece, bf16),
        in_specs=[SMEM, VMEM, VMEM],
        out_specs=VMEM,
        compiler_params=small(),
    )(source, own, foreign)
    pairs = lax.all_to_all(pairs, "head", 0, 0, tiled=True, axis_index_groups=kv_groups)
    pairs = pairs.reshape((group, per_rank * slot_count) + piece)

    done = pl.pallas_call(
        functools.partial(attend, per_span),
        out_shape=jax.ShapeDtypeStruct((group, per_rank * BLK, width), bf16),
        in_specs=[SMEM, SMEM, SMEM] + [VMEM] * (chips + 1),
        out_specs=VMEM,
        scratch_shapes=[pltpu.VMEM((per_rank, slot_count * BLK, width), bf16)] * 2,
        compiler_params=small(24),
    )(me[None], rank[None], span_order, *query_here, pairs)

    out = lax.all_to_all(done, "head", 0, 0, tiled=True, axis_index_groups=kv_groups)
    return out.reshape(rows_device, 1, width)


def solution(mesh):
    in_specs = (
        P("ctx", "head", None),
        P(("ctx", "head"), None, None),
        P(("ctx", "head"), None, None),
        P(),
        P(),
    )
    out_specs = P("ctx", "head", None)
    return jax.shard_map(body, mesh=mesh, in_specs=in_specs, out_specs=out_specs, check_vma=False)
```

```python
import functools

import jax
import jax.numpy as jnp
from jax import lax
from jax.experimental import pallas as pl
from jax.experimental.pallas import tpu as pltpu
from jax.sharding import PartitionSpec as P

BLK = 128
CAP = 2
LOG2E = 1.4426950408889634
MASKED = -1e30
SMEM = pl.BlockSpec(memory_space=pltpu.SMEM)
VMEM = pl.BlockSpec(memory_space=pltpu.VMEM)


def small(mib=4):
    return pltpu.CompilerParams(vmem_limit_bytes=mib * 2**20)


def asked_range(per_span, me_ref, span_ref, listed_ref, out_ref):
    listed = listed_ref[...]
    slots, positions = listed.shape
    first = span_ref[2 * me_ref[0]]
    second = span_ref[2 * me_ref[0] + 1]
    slot = lax.broadcasted_iota(jnp.int32, listed.shape, 0)
    position = lax.broadcasted_iota(jnp.int32, listed.shape, 1)
    span = listed // per_span
    mine = (slot <= position) & ((span == first) | (span == second))
    block = listed % per_span + jnp.where(span == second, per_span, 0)
    low = jnp.min(jnp.where(mine, block, 2 * per_span - 1), axis=0, keepdims=True)
    high = jnp.max(jnp.where(mine, block, 0), axis=0, keepdims=True)
    low = jnp.broadcast_to(low, (8, positions))
    high = jnp.broadcast_to(high, (8, positions))
    step = 1
    while step < per_span:
        low = jnp.minimum(low, pltpu.roll(low, positions - step, 1))
        high = jnp.maximum(high, pltpu.roll(high, positions - step, 1))
        step *= 2
    out_ref[0:1, :] = low[0:1]
    out_ref[1:2, :] = high[0:1]


def pick_asked(per_span, span_ref, range_ref, own_ref, out_ref):
    for d in range(out_ref.shape[0] // CAP):
        a = span_ref[2 * d] * per_span
        b = span_ref[2 * d + 1] * per_span
        out_ref[2 * d] = own_ref[jnp.minimum(range_ref[0, a], range_ref[0, b])]
        out_ref[2 * d + 1] = own_ref[jnp.maximum(range_ref[1, a], range_ref[1, b])]


def find_sources(per_span, me_ref, span_ref, listed_ref, out_ref, inverse, lowest, owners, helds):
    me = me_ref[0]
    slots = listed_ref.shape[0]
    span_count = span_ref.shape[0]
    blocks = 2 * per_span

    def invert(s, carry):
        inverse[span_ref[s]] = s
        return carry

    def reset(s, carry):
        lowest[s] = blocks
        return carry

    lax.fori_loop(0, span_count, invert, 0, unroll=4)
    lax.fori_loop(0, span_count // 2, reset, 0, unroll=4)

    def scan(block, carry):
        position = span_ref[2 * me + block // per_span] * per_span + block % per_span
        for j in range(1, slots):
            name = listed_ref[j, position]
            at = inverse[name // per_span]
            owner = at // 2
            held = at % 2 * per_span + name % per_span
            owners[block * slots + j] = owner
            helds[block * slots + j] = held
            lowest[owner] = jnp.minimum(lowest[owner], jnp.where(j <= position, held, blocks))
        return carry

    lax.fori_loop(0, blocks, scan, 0, unroll=2)

    def place(block, carry):
        out_ref[block * slots] = block
        for j in range(1, slots):
            owner = owners[block * slots + j]
            held = helds[block * slots + j]
            foreign = blocks + CAP * owner + jnp.where(held > lowest[owner], 1, 0)
            out_ref[block * slots + j] = jnp.where(owner == me, held, foreign)
        return carry

    lax.fori_loop(0, blocks, place, 0, unroll=2)


def pick_pairs(source_ref, own_ref, foreign_ref, out_ref):
    own_count = own_ref.shape[0]
    for i in range(out_ref.shape[0]):
        at = source_ref[i]
        mine = own_ref[jnp.minimum(at, own_count - 1)]
        theirs = foreign_ref[jnp.maximum(at - own_count, 0)]
        out_ref[i] = jnp.where(at < own_count, mine, theirs)


def bundle(rank_ref, query_ref, sibling_ref, *out_refs):
    chip = rank_ref[0] // 2
    core = rank_ref[0] % 2
    for k, out_ref in enumerate(out_refs):
        to = chip ^ k
        out_ref[0] = query_ref[2 * to + core]
        out_ref[1] = sibling_ref[to]


def attend(per_span, me_ref, rank_ref, span_ref, *refs):
    *query_refs, pair_ref, out_ref, key_all, value_all = refs
    pieces, pair_count, _, rows, width = pair_ref.shape
    blocks = key_all.shape[0]
    slots = pair_count // blocks
    factor = (width ** -0.5) * LOG2E
    chip = rank_ref[0] // 2
    core = rank_ref[0] % 2
    row = lax.broadcasted_iota(jnp.int32, (BLK, BLK), 0)
    col = lax.broadcasted_iota(jnp.int32, (BLK, BLK), 1)
    piece = col // rows
    half = pieces // 2
    causal = 2 * rows * (piece % half) + rows * (piece // half) + col % rows <= row
    causal = jnp.concatenate([causal, causal], axis=0)
    for b in range(blocks):
        for j in range(slots):
            i = b * slots + j
            key_all[b, j * BLK:(j + 1) * BLK, :] = pair_ref[:, i, 0].reshape(BLK, width)
            value_all[b, j * BLK:(j + 1) * BLK, :] = pair_ref[:, i, 1].reshape(BLK, width)
    for b in range(blocks):
        block = rank_ref[0] * blocks + b
        position = span_ref[2 * me_ref[0] + block // per_span] * per_span + block % per_span
        here = slice(b * BLK, (b + 1) * BLK)
        for k, query_ref in enumerate(query_refs):
            q = query_ref[:, here, :].reshape(2 * BLK, width)
            s = lax.dot_general(
                q, key_all[b], (((1,), (1,)), ((), ())), preferred_element_type=jnp.float32
            )
            parts = [jnp.where(causal, s[:, :BLK], MASKED)]
            for j in range(1, slots):
                parts.append(jnp.where(position >= j, s[:, j * BLK:(j + 1) * BLK], MASKED))
            peak = functools.reduce(jnp.maximum, parts)
            peak = jnp.max(peak, axis=1, keepdims=True) * factor
            total = jnp.zeros((2 * BLK, BLK), jnp.float32)
            mixed = jnp.zeros((2 * BLK, width), jnp.float32)
            for j in range(slots):
                raised = jnp.exp2(parts[j] * factor - peak)
                total += raised
                mixed += jnp.dot(
                    raised.astype(jnp.bfloat16),
                    value_all[b, j * BLK:(j + 1) * BLK],
                    preferred_element_type=jnp.float32,
                )
            total = jnp.sum(total, axis=1, keepdims=True)
            result = (mixed * (1.0 / total)).astype(jnp.bfloat16)
            out_ref[2 * (chip ^ k) + core, here, :] = result[:BLK]
            out_ref[2 * (chip ^ k) + 1 - core, here, :] = result[BLK:]


def body(queries, keys, values, key_blocks, span_order):
    ctx_count = lax.axis_size("ctx")
    head_count = lax.axis_size("head")
    rows_device, _, width = queries.shape
    shard_rows, kv_heads, _ = keys.shape
    slot_count = key_blocks.shape[1]
    block_count = rows_device // BLK
    per_span = block_count // 2
    group = head_count // kv_heads
    shards_per_block = BLK // shard_rows
    halves = group // shards_per_block
    piece_rows = shard_rows // halves
    per_rank = block_count // group
    chips = group // 2
    i32 = jnp.int32
    bf16 = jnp.bfloat16
    me = lax.axis_index("ctx").astype(i32)
    rank = lax.rem(lax.axis_index("head").astype(i32), group)
    piece = (2, piece_rows, width)
    listed = key_blocks.T

    core = lax.rem(rank, 2)
    query_parts = queries.reshape(chips, 2, rows_device // group, width)
    crossing = lax.dynamic_index_in_dim(query_parts, 1 - core, 1, keepdims=False)
    sibling = lax.ppermute(crossing, "head", [(i, i ^ 1) for i in range(head_count)])
    part = jax.ShapeDtypeStruct((2, rows_device // group, width), bf16)
    bundles = pl.pallas_call(
        bundle,
        out_shape=(part,) * chips,
        in_specs=[SMEM, VMEM, VMEM],
        out_specs=(VMEM,) * chips,
        compiler_params=small(8),
    )(rank[None], query_parts.reshape(group, rows_device // group, width), sibling)

    spread_groups = [
        [shards_per_block * j + q for j in range(block_count)] for q in range(shards_per_block)
    ]
    kv = jnp.stack([keys, values])
    kv = kv.reshape(2, halves, piece_rows, kv_heads, width).transpose(3, 1, 0, 2, 4)
    kv = kv.reshape((block_count,) + piece)
    kv, bundles = lax.optimization_barrier((kv, bundles))
    own = lax.all_to_all(kv, "head", 0, 0, tiled=True, axis_index_groups=spread_groups)

    ranges = pl.pallas_call(
        functools.partial(asked_range, per_span),
        out_shape=jax.ShapeDtypeStruct((2, key_blocks.shape[0]), i32),
        in_specs=[SMEM, SMEM, VMEM],
        out_specs=VMEM,
        compiler_params=small(),
    )(me[None], span_order, listed)

    asked = pl.pallas_call(
        functools.partial(pick_asked, per_span),
        out_shape=jax.ShapeDtypeStruct((ctx_count * CAP,) + piece, bf16),
        in_specs=[SMEM, SMEM, VMEM],
        out_specs=VMEM,
        compiler_params=small(),
    )(span_order, ranges, own)
    foreign = lax.all_to_all(asked, "ctx", 0, 0, tiled=True)

    *bundles, span_after, _ = lax.optimization_barrier((*bundles, span_order, asked))
    query_here = [bundles[0]] + [
        lax.ppermute(bundles[k], "head", [(i, i ^ (2 * k)) for i in range(head_count)])
        for k in range(1, chips)
    ]
    source = pl.pallas_call(
        functools.partial(find_sources, per_span),
        out_shape=jax.ShapeDtypeStruct((block_count * slot_count,), i32),
        in_specs=[SMEM, SMEM, SMEM],
        out_specs=SMEM,
        scratch_shapes=[
            pltpu.SMEM((2 * ctx_count,), i32),
            pltpu.SMEM((ctx_count,), i32),
            pltpu.SMEM((block_count * slot_count,), i32),
            pltpu.SMEM((block_count * slot_count,), i32),
        ],
        compiler_params=small(),
    )(me[None], span_after, listed)

    kv_groups = [[g * group + i for i in range(group)] for g in range(kv_heads)]
    source, foreign, query_here = lax.optimization_barrier((source, foreign, query_here))
    pairs = pl.pallas_call(
        pick_pairs,
        out_shape=jax.ShapeDtypeStruct((block_count * slot_count,) + piece, bf16),
        in_specs=[SMEM, VMEM, VMEM],
        out_specs=VMEM,
        compiler_params=small(),
    )(source, own, foreign)
    pairs = lax.all_to_all(pairs, "head", 0, 0, tiled=True, axis_index_groups=kv_groups)
    pairs = pairs.reshape((group, per_rank * slot_count) + piece)

    done = pl.pallas_call(
        functools.partial(attend, per_span),
        out_shape=jax.ShapeDtypeStruct((group, per_rank * BLK, width), bf16),
        in_specs=[SMEM, SMEM, SMEM] + [VMEM] * (chips + 1),
        out_specs=VMEM,
        scratch_shapes=[pltpu.VMEM((per_rank, slot_count * BLK, width), bf16)] * 2,
        compiler_params=small(24),
    )(me[None], rank[None], span_order, *query_here, pairs)

    out = lax.all_to_all(done, "head", 0, 0, tiled=True, axis_index_groups=kv_groups)
    return out.reshape(rows_device, 1, width)


def solution(mesh):
    in_specs = (
        P("ctx", "head", None),
        P(("ctx", "head"), None, None),
        P(("ctx", "head"), None, None),
        P(),
        P(),
    )
    out_specs = P("ctx", "head", None)
    return jax.shard_map(body, mesh=mesh, in_specs=in_specs, out_specs=out_specs, check_vma=False)
```

```python
import functools

import jax
import jax.numpy as jnp
from jax import lax
from jax.experimental import pallas as pl
from jax.experimental.pallas import tpu as pltpu
from jax.sharding import PartitionSpec as P

BLK = 128
CAP = 2
LOG2E = 1.4426950408889634
MASKED = -1e30
SMEM = pl.BlockSpec(memory_space=pltpu.SMEM)
VMEM = pl.BlockSpec(memory_space=pltpu.VMEM)


def small(mib=4):
    return pltpu.CompilerParams(vmem_limit_bytes=mib * 2**20)


def tables(per_span, me_ref, span_ref, listed_ref, out_ref):
    listed = listed_ref[...]
    slots, positions = listed.shape
    span_count = span_ref.shape[0]
    blocks = 2 * per_span
    me = me_ref[0]
    first = span_ref[2 * me]
    second = span_ref[2 * me + 1]
    slot = lax.broadcasted_iota(jnp.int32, listed.shape, 0)
    position = lax.broadcasted_iota(jnp.int32, listed.shape, 1)
    used = slot <= position
    span = listed // per_span
    rest = listed % per_span

    mine = used & ((span == first) | (span == second))
    block = rest + jnp.where(span == second, per_span, 0)
    low = jnp.min(jnp.where(mine, block, blocks - 1), axis=0, keepdims=True)
    high = jnp.max(jnp.where(mine, block, 0), axis=0, keepdims=True)
    low = jnp.broadcast_to(low, (8, positions))
    high = jnp.broadcast_to(high, (8, positions))
    step = 1
    while step < per_span:
        low = jnp.minimum(low, pltpu.roll(low, positions - step, 1))
        high = jnp.maximum(high, pltpu.roll(high, positions - step, 1))
        step *= 2
    out_ref[0:1, :] = low[0:1]
    out_ref[1:2, :] = high[0:1]

    at = jnp.zeros_like(listed)
    for s in range(span_count):
        at = jnp.where(span == span_ref[s], s, at)
    owner = at // 2
    held = at % 2 * per_span + rest
    asker = position // per_span
    asking = used & ((asker == first) | (asker == second))
    held_float = held.astype(jnp.float32)
    lowest = jnp.zeros(listed.shape, jnp.float32)
    for o in range(span_count // 2):
        here = owner == o
        least = jnp.where(here & asking, held_float, float(blocks))
        least = jnp.min(jnp.min(least, axis=0, keepdims=True), axis=1, keepdims=True)
        lowest = jnp.where(here, least, lowest)
    foreign = blocks + CAP * owner + jnp.where(held_float > lowest, 1, 0)
    out_ref[2:2 + slots, :] = jnp.where(owner == me, held, foreign)


def pick_asked(per_span, span_ref, table_ref, own_ref, out_ref):
    for d in range(out_ref.shape[0] // CAP):
        a = span_ref[2 * d] * per_span
        b = span_ref[2 * d + 1] * per_span
        out_ref[2 * d] = own_ref[jnp.minimum(table_ref[0, a], table_ref[0, b])]
        out_ref[2 * d + 1] = own_ref[jnp.maximum(table_ref[1, a], table_ref[1, b])]


def pick_pairs(per_span, me_ref, span_ref, table_ref, own_ref, foreign_ref, out_ref):
    own_count = own_ref.shape[0]
    slots = out_ref.shape[0] // own_count
    for block in range(own_count):
        position = span_ref[2 * me_ref[0] + block // per_span] * per_span + block % per_span
        for j in range(slots):
            at = table_ref[2 + j, position]
            mine = own_ref[jnp.minimum(at, own_count - 1)]
            theirs = foreign_ref[jnp.maximum(at - own_count, 0)]
            out_ref[block * slots + j] = jnp.where(at < own_count, mine, theirs)


def bundle(rank_ref, query_ref, sibling_ref, *out_refs):
    chip = rank_ref[0] // 2
    core = rank_ref[0] % 2
    for k, out_ref in enumerate(out_refs):
        to = chip ^ k
        out_ref[0] = query_ref[2 * to + core]
        out_ref[1] = sibling_ref[to]


def attend(per_span, me_ref, rank_ref, span_ref, *refs):
    *query_refs, pair_ref, out_ref, key_all, value_all = refs
    pieces, pair_count, _, rows, width = pair_ref.shape
    blocks = key_all.shape[0]
    slots = pair_count // blocks
    factor = (width ** -0.5) * LOG2E
    chip = rank_ref[0] // 2
    core = rank_ref[0] % 2
    row = lax.broadcasted_iota(jnp.int32, (BLK, BLK), 0)
    col = lax.broadcasted_iota(jnp.int32, (BLK, BLK), 1)
    piece = col // rows
    half = pieces // 2
    causal = 2 * rows * (piece % half) + rows * (piece // half) + col % rows <= row
    causal = jnp.concatenate([causal, causal], axis=0)
    for b in range(blocks):
        for j in range(slots):
            i = b * slots + j
            key_all[b, j * BLK:(j + 1) * BLK, :] = pair_ref[:, i, 0].reshape(BLK, width)
            value_all[b, j * BLK:(j + 1) * BLK, :] = pair_ref[:, i, 1].reshape(BLK, width)
    for b in range(blocks):
        block = rank_ref[0] * blocks + b
        position = span_ref[2 * me_ref[0] + block // per_span] * per_span + block % per_span
        here = slice(b * BLK, (b + 1) * BLK)
        for k, query_ref in enumerate(query_refs):
            q = query_ref[:, here, :].reshape(2 * BLK, width)
            s = lax.dot_general(
                q, key_all[b], (((1,), (1,)), ((), ())), preferred_element_type=jnp.float32
            )
            parts = [jnp.where(causal, s[:, :BLK], MASKED)]
            for j in range(1, slots):
                parts.append(jnp.where(position >= j, s[:, j * BLK:(j + 1) * BLK], MASKED))
            peak = functools.reduce(jnp.maximum, parts)
            peak = jnp.max(peak, axis=1, keepdims=True) * factor
            total = jnp.zeros((2 * BLK, BLK), jnp.float32)
            mixed = jnp.zeros((2 * BLK, width), jnp.float32)
            for j in range(slots):
                raised = jnp.exp2(parts[j] * factor - peak)
                total += raised
                mixed += jnp.dot(
                    raised.astype(jnp.bfloat16),
                    value_all[b, j * BLK:(j + 1) * BLK],
                    preferred_element_type=jnp.float32,
                )
            total = jnp.sum(total, axis=1, keepdims=True)
            result = (mixed * (1.0 / total)).astype(jnp.bfloat16)
            out_ref[2 * (chip ^ k) + core, here, :] = result[:BLK]
            out_ref[2 * (chip ^ k) + 1 - core, here, :] = result[BLK:]


def body(queries, keys, values, key_blocks, span_order):
    ctx_count = lax.axis_size("ctx")
    head_count = lax.axis_size("head")
    rows_device, _, width = queries.shape
    shard_rows, kv_heads, _ = keys.shape
    slot_count = key_blocks.shape[1]
    block_count = rows_device // BLK
    per_span = block_count // 2
    group = head_count // kv_heads
    shards_per_block = BLK // shard_rows
    halves = group // shards_per_block
    piece_rows = shard_rows // halves
    per_rank = block_count // group
    chips = group // 2
    i32 = jnp.int32
    bf16 = jnp.bfloat16
    me = lax.axis_index("ctx").astype(i32)
    rank = lax.rem(lax.axis_index("head").astype(i32), group)
    piece = (2, piece_rows, width)
    listed = key_blocks.T

    spread_groups = [
        [shards_per_block * j + q for j in range(block_count)] for q in range(shards_per_block)
    ]
    kv = jnp.stack([keys, values])
    kv = kv.reshape(2, halves, piece_rows, kv_heads, width).transpose(3, 1, 0, 2, 4)
    kv = kv.reshape((block_count,) + piece)
    kv, listed, queries = lax.optimization_barrier((kv, listed, queries))
    own = lax.all_to_all(kv, "head", 0, 0, tiled=True, axis_index_groups=spread_groups)

    table = pl.pallas_call(
        functools.partial(tables, per_span),
        out_shape=jax.ShapeDtypeStruct((2 + slot_count, key_blocks.shape[0]), i32),
        in_specs=[SMEM, SMEM, VMEM],
        out_specs=VMEM,
        compiler_params=small(),
        cost_estimate=pl.CostEstimate(flops=2 * 10**10, bytes_accessed=2**14, transcendentals=0),
    )(me[None], span_order, listed)

    core = lax.rem(rank, 2)
    query_parts = queries.reshape(chips, 2, rows_device // group, width)
    crossing = lax.dynamic_index_in_dim(query_parts, 1 - core, 1, keepdims=False)
    sibling = lax.ppermute(crossing, "head", [(i, i ^ 1) for i in range(head_count)])
    part = jax.ShapeDtypeStruct((2, rows_device // group, width), bf16)
    bundles = pl.pallas_call(
        bundle,
        out_shape=(part,) * chips,
        in_specs=[SMEM, VMEM, VMEM],
        out_specs=(VMEM,) * chips,
        compiler_params=small(8),
    )(rank[None], query_parts.reshape(group, rows_device // group, width), sibling)

    own, table, bundles = lax.optimization_barrier((own, table, bundles))

    asked = pl.pallas_call(
        functools.partial(pick_asked, per_span),
        out_shape=jax.ShapeDtypeStruct((ctx_count * CAP,) + piece, bf16),
        in_specs=[SMEM, SMEM, VMEM],
        out_specs=VMEM,
        compiler_params=small(),
    )(span_order, table, own)
    foreign = lax.all_to_all(asked, "ctx", 0, 0, tiled=True)

    *bundles, _ = lax.optimization_barrier((*bundles, asked))
    near, *far = [
        lax.ppermute(bundles[k], "head", [(i, i ^ (2 * k)) for i in range(head_count)])
        for k in range(1, chips)
    ]

    kv_groups = [[g * group + i for i in range(group)] for g in range(kv_heads)]
    foreign, far = lax.optimization_barrier((foreign, far))
    query_here = [bundles[0], near, *far]
    pairs = pl.pallas_call(
        functools.partial(pick_pairs, per_span),
        out_shape=jax.ShapeDtypeStruct((block_count * slot_count,) + piece, bf16),
        in_specs=[SMEM, SMEM, SMEM, VMEM, VMEM],
        out_specs=VMEM,
        compiler_params=small(),
    )(me[None], span_order, table, own, foreign)
    pairs = lax.all_to_all(pairs, "head", 0, 0, tiled=True, axis_index_groups=kv_groups)
    pairs = pairs.reshape((group, per_rank * slot_count) + piece)

    done = pl.pallas_call(
        functools.partial(attend, per_span),
        out_shape=jax.ShapeDtypeStruct((group, per_rank * BLK, width), bf16),
        in_specs=[SMEM, SMEM, SMEM] + [VMEM] * (chips + 1),
        out_specs=VMEM,
        scratch_shapes=[pltpu.VMEM((per_rank, slot_count * BLK, width), bf16)] * 2,
        compiler_params=small(24),
    )(me[None], rank[None], span_order, *query_here, pairs)

    out = lax.all_to_all(done, "head", 0, 0, tiled=True, axis_index_groups=kv_groups)
    return out.reshape(rows_device, 1, width)


def solution(mesh):
    in_specs = (
        P("ctx", "head", None),
        P(("ctx", "head"), None, None),
        P(("ctx", "head"), None, None),
        P(),
        P(),
    )
    out_specs = P("ctx", "head", None)
    return jax.shard_map(body, mesh=mesh, in_specs=in_specs, out_specs=out_specs, check_vma=False)
```

```python
import functools

import jax
import jax.numpy as jnp
from jax import lax
from jax.experimental import pallas as pl
from jax.experimental.pallas import tpu as pltpu
from jax.sharding import PartitionSpec as P

BLK = 128
CAP = 2
LOG2E = 1.4426950408889634
MASKED = -1e30
SMEM = pl.BlockSpec(memory_space=pltpu.SMEM)
VMEM = pl.BlockSpec(memory_space=pltpu.VMEM)


def small(mib=4):
    return pltpu.CompilerParams(vmem_limit_bytes=mib * 2**20)


def pack(key_ref, value_ref, out_ref):
    heads, halves, _, rows, width = out_ref.shape
    for i, ref in enumerate((key_ref, value_ref)):
        turned = jnp.swapaxes(ref[...].astype(jnp.float32), 0, 1).astype(jnp.bfloat16)
        out_ref[:, :, i] = turned.reshape(heads, halves, rows, width)


def tables(per_span, me_ref, span_ref, listed_ref, out_ref):
    listed = listed_ref[...]
    slots, positions = listed.shape
    span_count = span_ref.shape[0]
    blocks = 2 * per_span
    me = me_ref[0]
    first = span_ref[2 * me]
    second = span_ref[2 * me + 1]
    slot = lax.broadcasted_iota(jnp.int32, listed.shape, 0)
    position = lax.broadcasted_iota(jnp.int32, listed.shape, 1)
    used = slot <= position
    span = listed // per_span
    rest = listed % per_span

    mine = used & ((span == first) | (span == second))
    block = rest + jnp.where(span == second, per_span, 0)
    low = jnp.min(jnp.where(mine, block, blocks - 1), axis=0, keepdims=True)
    high = jnp.max(jnp.where(mine, block, 0), axis=0, keepdims=True)
    low = jnp.broadcast_to(low, (8, positions))
    high = jnp.broadcast_to(high, (8, positions))
    step = 1
    while step < per_span:
        low = jnp.minimum(low, pltpu.roll(low, positions - step, 1))
        high = jnp.maximum(high, pltpu.roll(high, positions - step, 1))
        step *= 2
    out_ref[0:1, :] = low[0:1]
    out_ref[1:2, :] = high[0:1]

    at = jnp.zeros_like(listed)
    for s in range(span_count):
        at = jnp.where(span == span_ref[s], s, at)
    owner = at // 2
    held = at % 2 * per_span + rest
    asker = position // per_span
    asking = used & ((asker == first) | (asker == second))
    held_float = held.astype(jnp.float32)
    lowest = jnp.zeros(listed.shape, jnp.float32)
    for o in range(span_count // 2):
        here = owner == o
        least = jnp.where(here & asking, held_float, float(blocks))
        least = jnp.min(jnp.min(least, axis=0, keepdims=True), axis=1, keepdims=True)
        lowest = jnp.where(here, least, lowest)
    foreign = blocks + CAP * owner + jnp.where(held_float > lowest, 1, 0)
    out_ref[2:2 + slots, :] = jnp.where(owner == me, held, foreign)


def pick_asked(per_span, span_ref, table_ref, own_ref, out_ref):
    for d in range(out_ref.shape[0] // CAP):
        a = span_ref[2 * d] * per_span
        b = span_ref[2 * d + 1] * per_span
        out_ref[2 * d] = own_ref[jnp.minimum(table_ref[0, a], table_ref[0, b])]
        out_ref[2 * d + 1] = own_ref[jnp.maximum(table_ref[1, a], table_ref[1, b])]


def pick_pairs(per_span, me_ref, span_ref, table_ref, own_ref, foreign_ref, out_ref):
    own_count = own_ref.shape[0]
    slots = out_ref.shape[0] // own_count
    for block in range(own_count):
        position = span_ref[2 * me_ref[0] + block // per_span] * per_span + block % per_span
        for j in range(slots):
            at = table_ref[2 + j, position]
            mine = own_ref[jnp.minimum(at, own_count - 1)]
            theirs = foreign_ref[jnp.maximum(at - own_count, 0)]
            out_ref[block * slots + j] = jnp.where(at < own_count, mine, theirs)


def bundle(rank_ref, query_ref, sibling_ref, *out_refs):
    chip = rank_ref[0] // 2
    core = rank_ref[0] % 2
    for k, out_ref in enumerate(out_refs):
        to = chip ^ k
        out_ref[0] = query_ref[2 * to + core]
        out_ref[1] = sibling_ref[to]


def attend(per_span, me_ref, rank_ref, span_ref, *refs):
    *query_refs, pair_ref, out_ref, key_all, value_all = refs
    pieces, pair_count, _, rows, width = pair_ref.shape
    blocks = key_all.shape[0]
    slots = pair_count // blocks
    factor = (width ** -0.5) * LOG2E
    chip = rank_ref[0] // 2
    core = rank_ref[0] % 2
    row = lax.broadcasted_iota(jnp.int32, (BLK, BLK), 0)
    col = lax.broadcasted_iota(jnp.int32, (BLK, BLK), 1)
    piece = col // rows
    half = pieces // 2
    causal = 2 * rows * (piece % half) + rows * (piece // half) + col % rows <= row
    causal = jnp.concatenate([causal, causal], axis=0)
    for b in range(blocks):
        for j in range(slots):
            i = b * slots + j
            key_all[b, j * BLK:(j + 1) * BLK, :] = pair_ref[:, i, 0].reshape(BLK, width)
            value_all[b, j * BLK:(j + 1) * BLK, :] = pair_ref[:, i, 1].reshape(BLK, width)
    for b in range(blocks):
        block = rank_ref[0] * blocks + b
        position = span_ref[2 * me_ref[0] + block // per_span] * per_span + block % per_span
        here = slice(b * BLK, (b + 1) * BLK)
        for k, query_ref in enumerate(query_refs):
            q = query_ref[:, here, :].reshape(2 * BLK, width)
            s = lax.dot_general(
                q, key_all[b], (((1,), (1,)), ((), ())), preferred_element_type=jnp.float32
            )
            parts = [jnp.where(causal, s[:, :BLK], MASKED)]
            for j in range(1, slots):
                parts.append(jnp.where(position >= j, s[:, j * BLK:(j + 1) * BLK], MASKED))
            peak = functools.reduce(jnp.maximum, parts)
            peak = jnp.max(peak, axis=1, keepdims=True) * factor
            total = jnp.zeros((2 * BLK, BLK), jnp.float32)
            mixed = jnp.zeros((2 * BLK, width), jnp.float32)
            for j in range(slots):
                raised = jnp.exp2(parts[j] * factor - peak)
                total += raised
                mixed += jnp.dot(
                    raised.astype(jnp.bfloat16),
                    value_all[b, j * BLK:(j + 1) * BLK],
                    preferred_element_type=jnp.float32,
                )
            total = jnp.sum(total, axis=1, keepdims=True)
            result = (mixed * (1.0 / total)).astype(jnp.bfloat16)
            out_ref[2 * (chip ^ k) + core, here, :] = result[:BLK]
            out_ref[2 * (chip ^ k) + 1 - core, here, :] = result[BLK:]


def body(queries, keys, values, key_blocks, span_order):
    ctx_count = lax.axis_size("ctx")
    head_count = lax.axis_size("head")
    rows_device, _, width = queries.shape
    shard_rows, kv_heads, _ = keys.shape
    slot_count = key_blocks.shape[1]
    block_count = rows_device // BLK
    per_span = block_count // 2
    group = head_count // kv_heads
    shards_per_block = BLK // shard_rows
    halves = group // shards_per_block
    piece_rows = shard_rows // halves
    per_rank = block_count // group
    chips = group // 2
    i32 = jnp.int32
    bf16 = jnp.bfloat16
    me = lax.axis_index("ctx").astype(i32)
    rank = lax.rem(lax.axis_index("head").astype(i32), group)
    piece = (2, piece_rows, width)
    listed = key_blocks.T

    spread_groups = [
        [shards_per_block * j + q for j in range(block_count)] for q in range(shards_per_block)
    ]
    kv = pl.pallas_call(
        pack,
        out_shape=jax.ShapeDtypeStruct((kv_heads, halves) + piece, bf16),
        in_specs=[VMEM, VMEM],
        out_specs=VMEM,
        compiler_params=small(60),
    )(keys, values).reshape((block_count,) + piece)
    kv, listed, queries = lax.optimization_barrier((kv, listed, queries))
    own = lax.all_to_all(kv, "head", 0, 0, tiled=True, axis_index_groups=spread_groups)

    table = pl.pallas_call(
        functools.partial(tables, per_span),
        out_shape=jax.ShapeDtypeStruct((2 + slot_count, key_blocks.shape[0]), i32),
        in_specs=[SMEM, SMEM, VMEM],
        out_specs=VMEM,
        compiler_params=small(),
        cost_estimate=pl.CostEstimate(flops=2 * 10**10, bytes_accessed=2**14, transcendentals=0),
    )(me[None], span_order, listed)

    core = lax.rem(rank, 2)
    query_parts = queries.reshape(chips, 2, rows_device // group, width)
    crossing = lax.dynamic_index_in_dim(query_parts, 1 - core, 1, keepdims=False)
    sibling = lax.ppermute(crossing, "head", [(i, i ^ 1) for i in range(head_count)])
    part = jax.ShapeDtypeStruct((2, rows_device // group, width), bf16)
    bundles = pl.pallas_call(
        bundle,
        out_shape=(part,) * chips,
        in_specs=[SMEM, VMEM, VMEM],
        out_specs=(VMEM,) * chips,
        compiler_params=small(8),
    )(rank[None], query_parts.reshape(group, rows_device // group, width), sibling)

    own, table, bundles = lax.optimization_barrier((own, table, bundles))

    asked = pl.pallas_call(
        functools.partial(pick_asked, per_span),
        out_shape=jax.ShapeDtypeStruct((ctx_count * CAP,) + piece, bf16),
        in_specs=[SMEM, SMEM, VMEM],
        out_specs=VMEM,
        compiler_params=small(),
    )(span_order, table, own)
    foreign = lax.all_to_all(asked, "ctx", 0, 0, tiled=True)

    *bundles, _ = lax.optimization_barrier((*bundles, asked))
    arrived = {
        k: lax.ppermute(bundles[k], "head", [(i, i ^ (2 * k)) for i in range(head_count)])
        for k in (*range(2, chips), 1)
    }

    kv_groups = [[g * group + i for i in range(group)] for g in range(kv_heads)]
    foreign, arrived = lax.optimization_barrier((foreign, arrived))
    query_here = [bundles[0]] + [arrived[k] for k in range(1, chips)]
    pairs = pl.pallas_call(
        functools.partial(pick_pairs, per_span),
        out_shape=jax.ShapeDtypeStruct((block_count * slot_count,) + piece, bf16),
        in_specs=[SMEM, SMEM, SMEM, VMEM, VMEM],
        out_specs=VMEM,
        compiler_params=small(),
    )(me[None], span_order, table, own, foreign)
    pairs = lax.all_to_all(pairs, "head", 0, 0, tiled=True, axis_index_groups=kv_groups)
    pairs = pairs.reshape((group, per_rank * slot_count) + piece)

    done = pl.pallas_call(
        functools.partial(attend, per_span),
        out_shape=jax.ShapeDtypeStruct((group, per_rank * BLK, width), bf16),
        in_specs=[SMEM, SMEM, SMEM] + [VMEM] * (chips + 1),
        out_specs=VMEM,
        scratch_shapes=[pltpu.VMEM((per_rank, slot_count * BLK, width), bf16)] * 2,
        compiler_params=small(24),
    )(me[None], rank[None], span_order, *query_here, pairs)

    out = lax.all_to_all(done, "head", 0, 0, tiled=True, axis_index_groups=kv_groups)
    return out.reshape(rows_device, 1, width)


def solution(mesh):
    in_specs = (
        P("ctx", "head", None),
        P(("ctx", "head"), None, None),
        P(("ctx", "head"), None, None),
        P(),
        P(),
    )
    out_specs = P("ctx", "head", None)
    return jax.shard_map(body, mesh=mesh, in_specs=in_specs, out_specs=out_specs, check_vma=False)
```

```python
import functools

import jax
import jax.numpy as jnp
from jax import lax
from jax.experimental import pallas as pl
from jax.experimental.pallas import tpu as pltpu
from jax.sharding import PartitionSpec as P

BLK = 128
CAP = 2
LOG2E = 1.4426950408889634
MASKED = -1e30
SMEM = pl.BlockSpec(memory_space=pltpu.SMEM)
VMEM = pl.BlockSpec(memory_space=pltpu.VMEM)


def small(mib=4):
    return pltpu.CompilerParams(vmem_limit_bytes=mib * 2**20)


def pack(lead, key_ref, value_ref, out_ref):
    count, _, rows, width = out_ref.shape
    for i, ref in enumerate((key_ref, value_ref)):
        turned = jnp.swapaxes(ref[...].astype(jnp.float32), 0, 1).astype(jnp.bfloat16)
        turned = turned.reshape(count, rows, width)
        for j in range(count):
            out_ref[j ^ lead, i] = turned[j]


def tables(per_span, spread_lead, ctx_lead, me_ref, span_ref, listed_ref, out_ref):
    listed = listed_ref[...]
    slots, positions = listed.shape
    span_count = span_ref.shape[0]
    blocks = 2 * per_span
    me = me_ref[0]
    first = span_ref[2 * me]
    second = span_ref[2 * me + 1]
    slot = lax.broadcasted_iota(jnp.int32, listed.shape, 0)
    position = lax.broadcasted_iota(jnp.int32, listed.shape, 1)
    used = slot <= position
    span = listed // per_span
    rest = listed % per_span

    mine = used & ((span == first) | (span == second))
    block = rest + jnp.where(span == second, per_span, 0)
    low = jnp.min(jnp.where(mine, block, blocks - 1), axis=0, keepdims=True)
    high = jnp.max(jnp.where(mine, block, 0), axis=0, keepdims=True)
    low = jnp.broadcast_to(low, (8, positions))
    high = jnp.broadcast_to(high, (8, positions))
    step = 1
    while step < per_span:
        low = jnp.minimum(low, pltpu.roll(low, positions - step, 1))
        high = jnp.maximum(high, pltpu.roll(high, positions - step, 1))
        step *= 2
    out_ref[0:1, :] = low[0:1]
    out_ref[1:2, :] = high[0:1]

    at = jnp.zeros_like(listed)
    for s in range(span_count):
        at = jnp.where(span == span_ref[s], s, at)
    owner = at // 2
    held = at % 2 * per_span + rest
    asker = position // per_span
    asking = used & ((asker == first) | (asker == second))
    held_float = held.astype(jnp.float32)
    lowest = jnp.zeros(listed.shape, jnp.float32)
    for o in range(span_count // 2):
        here = owner == o
        least = jnp.where(here & asking, held_float, float(blocks))
        least = jnp.min(jnp.min(least, axis=0, keepdims=True), axis=1, keepdims=True)
        lowest = jnp.where(here, least, lowest)
    foreign = blocks + CAP * (owner ^ ctx_lead) + jnp.where(held_float > lowest, 1, 0)
    out_ref[2:2 + slots, :] = jnp.where(owner == me, held ^ spread_lead, foreign)


def pick_asked(per_span, spread_lead, ctx_lead, span_ref, table_ref, own_ref, out_ref):
    for d in range(out_ref.shape[0] // CAP):
        a = span_ref[2 * d] * per_span
        b = span_ref[2 * d + 1] * per_span
        low = jnp.minimum(table_ref[0, a], table_ref[0, b])
        high = jnp.maximum(table_ref[1, a], table_ref[1, b])
        out_ref[2 * (d ^ ctx_lead)] = own_ref[low ^ spread_lead]
        out_ref[2 * (d ^ ctx_lead) + 1] = own_ref[high ^ spread_lead]


def pick_pairs(per_span, me_ref, span_ref, table_ref, own_ref, foreign_ref, out_ref):
    own_count = own_ref.shape[0]
    slots = out_ref.shape[0] // own_count
    for block in range(own_count):
        position = span_ref[2 * me_ref[0] + block // per_span] * per_span + block % per_span
        for j in range(slots):
            at = table_ref[2 + j, position]
            mine = own_ref[jnp.minimum(at, own_count - 1)]
            theirs = foreign_ref[jnp.maximum(at - own_count, 0)]
            out_ref[block * slots + j] = jnp.where(at < own_count, mine, theirs)


def bundle(rank_ref, query_ref, sibling_ref, *out_refs):
    chip = rank_ref[0] // 2
    core = rank_ref[0] % 2
    for k, out_ref in enumerate(out_refs):
        to = chip ^ k
        out_ref[0] = query_ref[2 * to + core]
        out_ref[1] = sibling_ref[to]


def attend(per_span, lead, me_ref, rank_ref, span_ref, *refs):
    *query_refs, pair_ref, out_ref, key_all, value_all = refs
    pieces, pair_count, _, rows, width = pair_ref.shape
    blocks = key_all.shape[0]
    slots = pair_count // blocks
    factor = (width ** -0.5) * LOG2E
    chip = rank_ref[0] // 2
    core = rank_ref[0] % 2
    row = lax.broadcasted_iota(jnp.int32, (BLK, BLK), 0)
    col = lax.broadcasted_iota(jnp.int32, (BLK, BLK), 1)
    piece = (col // rows) ^ lead
    half = pieces // 2
    causal = 2 * rows * (piece % half) + rows * (piece // half) + col % rows <= row
    causal = jnp.concatenate([causal, causal], axis=0)
    for b in range(blocks):
        for j in range(slots):
            i = b * slots + j
            key_all[b, j * BLK:(j + 1) * BLK, :] = pair_ref[:, i, 0].reshape(BLK, width)
            value_all[b, j * BLK:(j + 1) * BLK, :] = pair_ref[:, i, 1].reshape(BLK, width)
    for b in range(blocks):
        block = rank_ref[0] * blocks + b
        position = span_ref[2 * me_ref[0] + block // per_span] * per_span + block % per_span
        here = slice(b * BLK, (b + 1) * BLK)
        for k, query_ref in enumerate(query_refs):
            q = query_ref[:, here, :].reshape(2 * BLK, width)
            s = lax.dot_general(
                q, key_all[b], (((1,), (1,)), ((), ())), preferred_element_type=jnp.float32
            )
            parts = [jnp.where(causal, s[:, :BLK], MASKED)]
            for j in range(1, slots):
                parts.append(jnp.where(position >= j, s[:, j * BLK:(j + 1) * BLK], MASKED))
            peak = functools.reduce(jnp.maximum, parts)
            peak = jnp.max(peak, axis=1, keepdims=True) * factor
            total = jnp.zeros((2 * BLK, BLK), jnp.float32)
            mixed = jnp.zeros((2 * BLK, width), jnp.float32)
            for j in range(slots):
                raised = jnp.exp2(parts[j] * factor - peak)
                total += raised
                mixed += jnp.dot(
                    raised.astype(jnp.bfloat16),
                    value_all[b, j * BLK:(j + 1) * BLK],
                    preferred_element_type=jnp.float32,
                )
            total = jnp.sum(total, axis=1, keepdims=True)
            result = (mixed * (1.0 / total)).astype(jnp.bfloat16)
            out_ref[2 * (chip ^ k) + core, here, :] = result[:BLK]
            out_ref[2 * (chip ^ k) + 1 - core, here, :] = result[BLK:]


def body(queries, keys, values, key_blocks, span_order):
    ctx_count = lax.axis_size("ctx")
    head_count = lax.axis_size("head")
    rows_device, _, width = queries.shape
    shard_rows, kv_heads, _ = keys.shape
    slot_count = key_blocks.shape[1]
    block_count = rows_device // BLK
    per_span = block_count // 2
    group = head_count // kv_heads
    shards_per_block = BLK // shard_rows
    halves = group // shards_per_block
    piece_rows = shard_rows // halves
    per_rank = block_count // group
    chips = group // 2
    i32 = jnp.int32
    bf16 = jnp.bfloat16
    me = lax.axis_index("ctx").astype(i32)
    spread_lead = block_count // 2 + block_count // 8
    ctx_lead = ctx_count // 2 + ctx_count // 4
    group_lead = 2
    rank = lax.rem(lax.axis_index("head").astype(i32), group) ^ group_lead
    piece = (2, piece_rows, width)
    listed = key_blocks.T

    spread_groups = [
        [shards_per_block * (j ^ spread_lead) + q for j in range(block_count)]
        for q in range(shards_per_block)
    ]
    kv = pl.pallas_call(
        functools.partial(pack, spread_lead),
        out_shape=jax.ShapeDtypeStruct((block_count,) + piece, bf16),
        in_specs=[VMEM, VMEM],
        out_specs=VMEM,
        compiler_params=small(60),
    )(keys, values)
    kv, listed, queries = lax.optimization_barrier((kv, listed, queries))
    own = lax.all_to_all(kv, "head", 0, 0, tiled=True, axis_index_groups=spread_groups)

    table = pl.pallas_call(
        functools.partial(tables, per_span, spread_lead, ctx_lead),
        out_shape=jax.ShapeDtypeStruct((2 + slot_count, key_blocks.shape[0]), i32),
        in_specs=[SMEM, SMEM, VMEM],
        out_specs=VMEM,
        compiler_params=small(),
        cost_estimate=pl.CostEstimate(flops=2 * 10**10, bytes_accessed=2**14, transcendentals=0),
    )(me[None], span_order, listed)

    core = lax.rem(rank, 2)
    query_parts = queries.reshape(chips, 2, rows_device // group, width)
    crossing = lax.dynamic_index_in_dim(query_parts, 1 - core, 1, keepdims=False)
    sibling = lax.ppermute(crossing, "head", [(i, i ^ 1) for i in range(head_count)])
    part = jax.ShapeDtypeStruct((2, rows_device // group, width), bf16)
    bundles = pl.pallas_call(
        bundle,
        out_shape=(part,) * chips,
        in_specs=[SMEM, VMEM, VMEM],
        out_specs=(VMEM,) * chips,
        compiler_params=small(8),
    )(rank[None], query_parts.reshape(group, rows_device // group, width), sibling)

    own, table, bundles = lax.optimization_barrier((own, table, bundles))

    asked = pl.pallas_call(
        functools.partial(pick_asked, per_span, spread_lead, ctx_lead),
        out_shape=jax.ShapeDtypeStruct((ctx_count * CAP,) + piece, bf16),
        in_specs=[SMEM, SMEM, VMEM],
        out_specs=VMEM,
        compiler_params=small(),
    )(span_order, table, own)
    ctx_groups = [[i ^ ctx_lead for i in range(ctx_count)]]
    foreign = lax.all_to_all(asked, "ctx", 0, 0, tiled=True, axis_index_groups=ctx_groups)

    *bundles, _ = lax.optimization_barrier((*bundles, asked))
    arrived = {
        k: lax.ppermute(bundles[k], "head", [(i, i ^ (2 * k)) for i in range(head_count)])
        for k in (*range(2, chips), 1)
    }

    kv_groups = [[g * group + (i ^ group_lead) for i in range(group)] for g in range(kv_heads)]
    foreign, arrived = lax.optimization_barrier((foreign, arrived))
    query_here = [bundles[0]] + [arrived[k] for k in range(1, chips)]
    pairs = pl.pallas_call(
        functools.partial(pick_pairs, per_span),
        out_shape=jax.ShapeDtypeStruct((block_count * slot_count,) + piece, bf16),
        in_specs=[SMEM, SMEM, SMEM, VMEM, VMEM],
        out_specs=VMEM,
        compiler_params=small(),
    )(me[None], span_order, table, own, foreign)
    pairs = lax.all_to_all(pairs, "head", 0, 0, tiled=True, axis_index_groups=kv_groups)
    pairs = pairs.reshape((group, per_rank * slot_count) + piece)

    done = pl.pallas_call(
        functools.partial(attend, per_span, group_lead),
        out_shape=jax.ShapeDtypeStruct((group, per_rank * BLK, width), bf16),
        in_specs=[SMEM, SMEM, SMEM] + [VMEM] * (chips + 1),
        out_specs=VMEM,
        scratch_shapes=[pltpu.VMEM((per_rank, slot_count * BLK, width), bf16)] * 2,
        compiler_params=small(24),
    )(me[None], rank[None], span_order, *query_here, pairs)

    out = lax.all_to_all(done, "head", 0, 0, tiled=True, axis_index_groups=kv_groups)
    return out.reshape(rows_device, 1, width)


def solution(mesh):
    in_specs = (
        P("ctx", "head", None),
        P(("ctx", "head"), None, None),
        P(("ctx", "head"), None, None),
        P(),
        P(),
    )
    out_specs = P("ctx", "head", None)
    return jax.shard_map(body, mesh=mesh, in_specs=in_specs, out_specs=out_specs, check_vma=False)
```

```python
import functools

import jax
import jax.numpy as jnp
from jax import lax
from jax.experimental import pallas as pl
from jax.experimental.pallas import tpu as pltpu
from jax.sharding import PartitionSpec as P

BLK = 128
CAP = 2
LOG2E = 1.4426950408889634
MASKED = -1e30
SMEM = pl.BlockSpec(memory_space=pltpu.SMEM)
VMEM = pl.BlockSpec(memory_space=pltpu.VMEM)


def small(mib=4):
    return pltpu.CompilerParams(vmem_limit_bytes=mib * 2**20)


def pack(lead, key_ref, value_ref, out_ref):
    count, _, rows, width = out_ref.shape
    for i, ref in enumerate((key_ref, value_ref)):
        turned = jnp.swapaxes(ref[...].astype(jnp.float32), 0, 1).astype(jnp.bfloat16)
        turned = turned.reshape(count, rows, width)
        for j in range(count):
            out_ref[j ^ lead, i] = turned[j]


def tables(per_span, spread_lead, ctx_lead, me_ref, span_ref, listed_ref, out_ref):
    listed = listed_ref[...]
    slots, positions = listed.shape
    span_count = span_ref.shape[0]
    blocks = 2 * per_span
    me = me_ref[0]
    first = span_ref[2 * me]
    second = span_ref[2 * me + 1]
    slot = lax.broadcasted_iota(jnp.int32, listed.shape, 0)
    position = lax.broadcasted_iota(jnp.int32, listed.shape, 1)
    used = slot <= position
    span = listed // per_span
    rest = listed % per_span

    mine = used & ((span == first) | (span == second))
    block = rest + jnp.where(span == second, per_span, 0)
    low = jnp.min(jnp.where(mine, block, blocks - 1), axis=0, keepdims=True)
    high = jnp.max(jnp.where(mine, block, 0), axis=0, keepdims=True)
    low = jnp.broadcast_to(low, (8, positions))
    high = jnp.broadcast_to(high, (8, positions))
    step = 1
    while step < per_span:
        low = jnp.minimum(low, pltpu.roll(low, positions - step, 1))
        high = jnp.maximum(high, pltpu.roll(high, positions - step, 1))
        step *= 2
    out_ref[0:1, :] = low[0:1]
    out_ref[1:2, :] = high[0:1]

    at = jnp.zeros_like(listed)
    for s in range(span_count):
        at = jnp.where(span == span_ref[s], s, at)
    owner = at // 2
    held = at % 2 * per_span + rest
    asker = position // per_span
    asking = used & ((asker == first) | (asker == second))
    held_float = held.astype(jnp.float32)
    lowest = jnp.zeros(listed.shape, jnp.float32)
    for o in range(span_count // 2):
        here = owner == o
        least = jnp.where(here & asking, held_float, float(blocks))
        least = jnp.min(jnp.min(least, axis=0, keepdims=True), axis=1, keepdims=True)
        lowest = jnp.where(here, least, lowest)
    foreign = blocks + CAP * (owner ^ ctx_lead) + jnp.where(held_float > lowest, 1, 0)
    out_ref[2:2 + slots, :] = jnp.where(owner == me, held ^ spread_lead, foreign)


def pick_asked(per_span, spread_lead, ctx_lead, span_ref, table_ref, own_ref, out_ref):
    for d in range(out_ref.shape[0] // CAP):
        a = span_ref[2 * d] * per_span
        b = span_ref[2 * d + 1] * per_span
        low = jnp.minimum(table_ref[0, a], table_ref[0, b])
        high = jnp.maximum(table_ref[1, a], table_ref[1, b])
        out_ref[2 * (d ^ ctx_lead)] = own_ref[low ^ spread_lead]
        out_ref[2 * (d ^ ctx_lead) + 1] = own_ref[high ^ spread_lead]


def pick_pairs(per_span, me_ref, span_ref, table_ref, own_ref, foreign_ref, out_ref):
    own_count = own_ref.shape[0]
    others = out_ref.shape[0] // own_count
    for block in range(own_count):
        position = span_ref[2 * me_ref[0] + block // per_span] * per_span + block % per_span
        for j in range(others):
            at = table_ref[3 + j, position]
            mine = own_ref[jnp.minimum(at, own_count - 1)]
            theirs = foreign_ref[jnp.maximum(at - own_count, 0)]
            out_ref[block * others + j] = jnp.where(at < own_count, mine, theirs)


def bundle(spread_lead, rank_ref, query_ref, sibling_ref, own_ref, *out_refs):
    chip = rank_ref[0] // 2
    core = rank_ref[0] % 2
    rows = query_ref.shape[1]
    _, _, piece_rows, _ = own_ref.shape
    per_chip = 2 * rows // BLK
    for k, out_ref in enumerate(out_refs):
        to = chip ^ k
        out_ref[0:rows] = query_ref[2 * to + core]
        out_ref[rows:2 * rows] = sibling_ref[to]
        for block in range(per_chip):
            for i in range(2):
                first = 2 * rows + (2 * block + i) * piece_rows
                out_ref[first:first + piece_rows] = own_ref[(per_chip * to + block) ^ spread_lead, i]


def cross(rank_ref, *refs):
    *bundle_refs, out_ref = refs
    each = out_ref.shape[0] // len(bundle_refs)
    first = bundle_refs[0].shape[0] - 2 * each
    theirs = pl.multiple_of(first + (1 - rank_ref[0] % 2) * each, 16)
    for k, ref in enumerate(bundle_refs):
        out_ref[k * each:(k + 1) * each] = ref[pl.ds(theirs, each)]


def attend(per_span, lead, me_ref, rank_ref, span_ref, *refs):
    *bundle_refs, crossed_ref, pair_ref, out_ref, key_all, value_all = refs
    pieces, pair_count, _, rows, width = pair_ref.shape
    blocks = key_all.shape[0]
    others = pair_count // blocks
    slots = others + 1
    half = pieces // 2
    factor = (width ** -0.5) * LOG2E
    chip = rank_ref[0] // 2
    core = rank_ref[0] % 2
    row = lax.broadcasted_iota(jnp.int32, (2 * BLK, BLK), 0)
    col = lax.broadcasted_iota(jnp.int32, (2 * BLK, BLK), 1)
    causal = col <= row % BLK
    each = 2 * rows * blocks
    query_rows = bundle_refs[0].shape[0] - 2 * each
    mine = query_rows + core * each
    for b in range(blocks):
        for k, ref in enumerate(bundle_refs):
            for from_core in range(2):
                g = (2 * (chip ^ k) + (core if from_core == 0 else 1 - core)) ^ lead
                to = pl.ds(pl.multiple_of(2 * rows * (g % half) + rows * (g // half), 16), rows)
                for i, store in enumerate((key_all, value_all)):
                    at = (2 * b + i) * rows
                    if from_core == 0:
                        store[b, to, :] = ref[pl.ds(pl.multiple_of(mine + at, 16), rows)]
                    else:
                        store[b, to, :] = crossed_ref[k * each + at:k * each + at + rows]
        for j in range(1, slots):
            i = b * others + j - 1
            key_all[b, j * BLK:(j + 1) * BLK, :] = pair_ref[:, i, 0].reshape(BLK, width)
            value_all[b, j * BLK:(j + 1) * BLK, :] = pair_ref[:, i, 1].reshape(BLK, width)
    for b in range(blocks):
        block = rank_ref[0] * blocks + b
        position = span_ref[2 * me_ref[0] + block // per_span] * per_span + block % per_span
        here = slice(b * BLK, (b + 1) * BLK)
        for k, ref in enumerate(bundle_refs):
            q = ref[0:query_rows].reshape(2, query_rows // 2, width)[:, here].reshape(2 * BLK, width)
            s = lax.dot_general(
                q, key_all[b], (((1,), (1,)), ((), ())), preferred_element_type=jnp.float32
            )
            parts = [jnp.where(causal, s[:, :BLK], MASKED)]
            for j in range(1, slots):
                parts.append(jnp.where(position >= j, s[:, j * BLK:(j + 1) * BLK], MASKED))
            peak = functools.reduce(jnp.maximum, parts)
            peak = jnp.max(peak, axis=1, keepdims=True) * factor
            total = jnp.zeros((2 * BLK, BLK), jnp.float32)
            mixed = jnp.zeros((2 * BLK, width), jnp.float32)
            for j in range(slots):
                raised = jnp.exp2(parts[j] * factor - peak)
                total += raised
                mixed += jnp.dot(
                    raised.astype(jnp.bfloat16),
                    value_all[b, j * BLK:(j + 1) * BLK],
                    preferred_element_type=jnp.float32,
                )
            total = jnp.sum(total, axis=1, keepdims=True)
            result = (mixed * (1.0 / total)).astype(jnp.bfloat16)
            out_ref[2 * (chip ^ k) + core, here, :] = result[:BLK]
            out_ref[2 * (chip ^ k) + 1 - core, here, :] = result[BLK:]


def body(queries, keys, values, key_blocks, span_order):
    ctx_count = lax.axis_size("ctx")
    head_count = lax.axis_size("head")
    rows_device, _, width = queries.shape
    shard_rows, kv_heads, _ = keys.shape
    slot_count = key_blocks.shape[1]
    block_count = rows_device // BLK
    per_span = block_count // 2
    group = head_count // kv_heads
    shards_per_block = BLK // shard_rows
    halves = group // shards_per_block
    piece_rows = shard_rows // halves
    per_rank = block_count // group
    chips = group // 2
    i32 = jnp.int32
    bf16 = jnp.bfloat16
    me = lax.axis_index("ctx").astype(i32)
    spread_lead = block_count // 2 + block_count // 8
    ctx_lead = ctx_count // 2 + ctx_count // 4
    group_lead = 2
    rank = lax.rem(lax.axis_index("head").astype(i32), group) ^ group_lead
    piece = (2, piece_rows, width)
    listed = key_blocks.T

    spread_groups = [
        [shards_per_block * (j ^ spread_lead) + q for j in range(block_count)]
        for q in range(shards_per_block)
    ]
    kv = pl.pallas_call(
        functools.partial(pack, spread_lead),
        out_shape=jax.ShapeDtypeStruct((block_count,) + piece, bf16),
        in_specs=[VMEM, VMEM],
        out_specs=VMEM,
        compiler_params=small(60),
    )(keys, values)
    kv, listed, queries = lax.optimization_barrier((kv, listed, queries))
    own = lax.all_to_all(kv, "head", 0, 0, tiled=True, axis_index_groups=spread_groups)

    table = pl.pallas_call(
        functools.partial(tables, per_span, spread_lead, ctx_lead),
        out_shape=jax.ShapeDtypeStruct((2 + slot_count, key_blocks.shape[0]), i32),
        in_specs=[SMEM, SMEM, VMEM],
        out_specs=VMEM,
        compiler_params=small(),
        cost_estimate=pl.CostEstimate(flops=2 * 10**10, bytes_accessed=2**14, transcendentals=0),
    )(me[None], span_order, listed)

    core = lax.rem(rank, 2)
    query_parts = queries.reshape(chips, 2, rows_device // group, width)
    crossing = lax.dynamic_index_in_dim(query_parts, 1 - core, 1, keepdims=False)
    sibling = lax.ppermute(crossing, "head", [(i, i ^ 1) for i in range(head_count)])
    own, table, sibling = lax.optimization_barrier((own, table, sibling))

    asked = pl.pallas_call(
        functools.partial(pick_asked, per_span, spread_lead, ctx_lead),
        out_shape=jax.ShapeDtypeStruct((ctx_count * CAP,) + piece, bf16),
        in_specs=[SMEM, SMEM, VMEM],
        out_specs=VMEM,
        compiler_params=small(),
    )(span_order, table, own)
    ctx_groups = [[i ^ ctx_lead for i in range(ctx_count)]]
    foreign = lax.all_to_all(asked, "ctx", 0, 0, tiled=True, axis_index_groups=ctx_groups)

    *parts, _ = lax.optimization_barrier((query_parts, sibling, own, asked))
    own_rows = 2 * per_rank * 2 * piece_rows
    part = jax.ShapeDtypeStruct((2 * (rows_device // group) + own_rows, width), bf16)
    bundles = pl.pallas_call(
        functools.partial(bundle, spread_lead),
        out_shape=(part,) * chips,
        in_specs=[SMEM, VMEM, VMEM, VMEM],
        out_specs=(VMEM,) * chips,
        compiler_params=small(8),
    )(rank[None], parts[0].reshape(group, rows_device // group, width), *parts[1:])
    arrived = [bundles[0]] + [
        lax.ppermute(bundles[k], "head", [(i, i ^ (2 * k)) for i in range(head_count)])
        for k in range(1, chips)
    ]

    kv_groups = [[g * group + (i ^ group_lead) for i in range(group)] for g in range(kv_heads)]
    foreign, arrived = lax.optimization_barrier((foreign, arrived))
    pairs = pl.pallas_call(
        functools.partial(pick_pairs, per_span),
        out_shape=jax.ShapeDtypeStruct((block_count * (slot_count - 1),) + piece, bf16),
        in_specs=[SMEM, SMEM, SMEM, VMEM, VMEM],
        out_specs=VMEM,
        compiler_params=small(),
    )(me[None], span_order, table, own, foreign)
    pairs, arrived = lax.optimization_barrier((pairs, arrived))
    pairs = lax.all_to_all(pairs, "head", 0, 0, tiled=True, axis_index_groups=kv_groups)
    pairs = pairs.reshape((group, per_rank * (slot_count - 1)) + piece)

    crossed = pl.pallas_call(
        cross,
        out_shape=jax.ShapeDtypeStruct((chips * own_rows // 2, width), bf16),
        in_specs=[SMEM] + [VMEM] * chips,
        out_specs=VMEM,
        compiler_params=small(8),
    )(rank[None], *arrived)
    crossed = lax.ppermute(crossed, "head", [(i, i ^ 1) for i in range(head_count)])

    done = pl.pallas_call(
        functools.partial(attend, per_span, group_lead),
        out_shape=jax.ShapeDtypeStruct((group, per_rank * BLK, width), bf16),
        in_specs=[SMEM, SMEM, SMEM] + [VMEM] * (chips + 2),
        out_specs=VMEM,
        scratch_shapes=[pltpu.VMEM((per_rank, slot_count * BLK, width), bf16)] * 2,
        compiler_params=small(24),
    )(me[None], rank[None], span_order, *arrived, crossed, pairs)

    out = lax.all_to_all(done, "head", 0, 0, tiled=True, axis_index_groups=kv_groups)
    return out.reshape(rows_device, 1, width)


def solution(mesh):
    in_specs = (
        P("ctx", "head", None),
        P(("ctx", "head"), None, None),
        P(("ctx", "head"), None, None),
        P(),
        P(),
    )
    out_specs = P("ctx", "head", None)
    return jax.shard_map(body, mesh=mesh, in_specs=in_specs, out_specs=out_specs, check_vma=False)
```

```python
import functools

import jax
import jax.numpy as jnp
from jax import lax
from jax.experimental import pallas as pl
from jax.experimental.pallas import tpu as pltpu
from jax.sharding import PartitionSpec as P

BLK = 128
CAP = 2
LOG2E = 1.4426950408889634
MASKED = -1e30
SMEM = pl.BlockSpec(memory_space=pltpu.SMEM)
VMEM = pl.BlockSpec(memory_space=pltpu.VMEM)


def small(mib=4):
    return pltpu.CompilerParams(vmem_limit_bytes=mib * 2**20)


def pack(lead, key_ref, value_ref, out_ref):
    count, _, rows, width = out_ref.shape
    for i, ref in enumerate((key_ref, value_ref)):
        turned = jnp.swapaxes(ref[...].astype(jnp.float32), 0, 1).astype(jnp.bfloat16)
        turned = turned.reshape(count, rows, width)
        for j in range(count):
            out_ref[j ^ lead, i] = turned[j]


def tables(per_span, spread_lead, ctx_lead, me_ref, span_ref, listed_ref, out_ref):
    listed = listed_ref[...]
    slots, positions = listed.shape
    span_count = span_ref.shape[0]
    blocks = 2 * per_span
    me = me_ref[0]
    first = span_ref[2 * me]
    second = span_ref[2 * me + 1]
    slot = lax.broadcasted_iota(jnp.int32, listed.shape, 0)
    position = lax.broadcasted_iota(jnp.int32, listed.shape, 1)
    used = slot <= position
    span = listed // per_span
    rest = listed % per_span

    mine = used & ((span == first) | (span == second))
    block = rest + jnp.where(span == second, per_span, 0)
    low = jnp.min(jnp.where(mine, block, blocks - 1), axis=0, keepdims=True)
    high = jnp.max(jnp.where(mine, block, 0), axis=0, keepdims=True)
    low = jnp.broadcast_to(low, (8, positions))
    high = jnp.broadcast_to(high, (8, positions))
    step = 1
    while step < per_span:
        low = jnp.minimum(low, pltpu.roll(low, positions - step, 1))
        high = jnp.maximum(high, pltpu.roll(high, positions - step, 1))
        step *= 2
    out_ref[0:1, :] = low[0:1]
    out_ref[1:2, :] = high[0:1]

    at = jnp.zeros_like(listed)
    for s in range(span_count):
        at = jnp.where(span == span_ref[s], s, at)
    owner = at // 2
    held = at % 2 * per_span + rest
    asker = position // per_span
    asking = used & ((asker == first) | (asker == second))
    held_float = held.astype(jnp.float32)
    lowest = jnp.zeros(listed.shape, jnp.float32)
    for o in range(span_count // 2):
        here = owner == o
        least = jnp.where(here & asking, held_float, float(blocks))
        least = jnp.min(jnp.min(least, axis=0, keepdims=True), axis=1, keepdims=True)
        lowest = jnp.where(here, least, lowest)
    foreign = blocks + CAP * (owner ^ ctx_lead) + jnp.where(held_float > lowest, 1, 0)
    out_ref[2:2 + slots, :] = jnp.where(owner == me, held ^ spread_lead, foreign)


def pick_asked(per_span, spread_lead, ctx_lead, span_ref, table_ref, own_ref, out_ref):
    for d in range(out_ref.shape[0] // CAP):
        a = span_ref[2 * d] * per_span
        b = span_ref[2 * d + 1] * per_span
        low = jnp.minimum(table_ref[0, a], table_ref[0, b])
        high = jnp.maximum(table_ref[1, a], table_ref[1, b])
        out_ref[2 * (d ^ ctx_lead)] = own_ref[low ^ spread_lead]
        out_ref[2 * (d ^ ctx_lead) + 1] = own_ref[high ^ spread_lead]


def pick_pairs(per_span, me_ref, span_ref, table_ref, own_ref, foreign_ref, out_ref):
    own_count = own_ref.shape[0]
    slots = out_ref.shape[0] // own_count
    for block in range(own_count):
        position = span_ref[2 * me_ref[0] + block // per_span] * per_span + block % per_span
        for j in range(slots):
            at = table_ref[2 + j, position]
            mine = own_ref[jnp.minimum(at, own_count - 1)]
            theirs = foreign_ref[jnp.maximum(at - own_count, 0)]
            out_ref[block * slots + j] = jnp.where(at < own_count, mine, theirs)


def bundle(rank_ref, query_ref, sibling_ref, *out_refs):
    chip = rank_ref[0] // 2
    core = rank_ref[0] % 2
    for k, out_ref in enumerate(out_refs):
        to = chip ^ k
        out_ref[0] = query_ref[2 * to + core]
        out_ref[1] = sibling_ref[to]


def attend(per_span, lead, me_ref, rank_ref, span_ref, *refs):
    *query_refs, pair_ref, out_ref, key_all, value_all = refs
    pieces, pair_count, _, rows, width = pair_ref.shape
    blocks = key_all.shape[0]
    slots = pair_count // blocks
    factor = (width ** -0.5) * LOG2E
    chip = rank_ref[0] // 2
    core = rank_ref[0] % 2
    row = lax.broadcasted_iota(jnp.int32, (BLK, BLK), 0)
    col = lax.broadcasted_iota(jnp.int32, (BLK, BLK), 1)
    piece = (col // rows) ^ lead
    half = pieces // 2
    causal = 2 * rows * (piece % half) + rows * (piece // half) + col % rows <= row
    causal = jnp.concatenate([causal, causal], axis=0)
    for b in range(blocks):
        for j in range(slots):
            i = b * slots + j
            key_all[b, j * BLK:(j + 1) * BLK, :] = pair_ref[:, i, 0].reshape(BLK, width)
            value_all[b, j * BLK:(j + 1) * BLK, :] = pair_ref[:, i, 1].reshape(BLK, width)
    for b in range(blocks):
        block = rank_ref[0] * blocks + b
        position = span_ref[2 * me_ref[0] + block // per_span] * per_span + block % per_span
        here = slice(b * BLK, (b + 1) * BLK)
        for k, query_ref in enumerate(query_refs):
            q = query_ref[:, here, :].reshape(2 * BLK, width)
            s = lax.dot_general(
                q, key_all[b], (((1,), (1,)), ((), ())), preferred_element_type=jnp.float32
            )
            parts = [jnp.where(causal, s[:, :BLK], MASKED)]
            for j in range(1, slots):
                parts.append(jnp.where(position >= j, s[:, j * BLK:(j + 1) * BLK], MASKED))
            peak = functools.reduce(jnp.maximum, parts)
            peak = jnp.max(peak, axis=1, keepdims=True) * factor
            total = jnp.zeros((2 * BLK, BLK), jnp.float32)
            mixed = jnp.zeros((2 * BLK, width), jnp.float32)
            for j in range(slots):
                raised = jnp.exp2(parts[j] * factor - peak)
                total += raised
                mixed += jnp.dot(
                    raised.astype(jnp.bfloat16),
                    value_all[b, j * BLK:(j + 1) * BLK],
                    preferred_element_type=jnp.float32,
                )
            total = jnp.sum(total, axis=1, keepdims=True)
            result = (mixed * (1.0 / total)).astype(jnp.bfloat16)
            out_ref[2 * (chip ^ k) + core, here, :] = result[:BLK]
            out_ref[2 * (chip ^ k) + 1 - core, here, :] = result[BLK:]


def body(queries, keys, values, key_blocks, span_order):
    ctx_count = lax.axis_size("ctx")
    head_count = lax.axis_size("head")
    rows_device, _, width = queries.shape
    shard_rows, kv_heads, _ = keys.shape
    slot_count = key_blocks.shape[1]
    block_count = rows_device // BLK
    per_span = block_count // 2
    group = head_count // kv_heads
    shards_per_block = BLK // shard_rows
    halves = group // shards_per_block
    piece_rows = shard_rows // halves
    per_rank = block_count // group
    chips = group // 2
    i32 = jnp.int32
    bf16 = jnp.bfloat16
    me = lax.axis_index("ctx").astype(i32)
    spread_lead = block_count // 2 + block_count // 8
    ctx_lead = ctx_count // 2 + ctx_count // 4
    group_lead = 2
    rank = lax.rem(lax.axis_index("head").astype(i32), group) ^ group_lead
    piece = (2, piece_rows, width)
    listed = key_blocks.T

    spread_groups = [
        [shards_per_block * (j ^ spread_lead) + q for j in range(block_count)]
        for q in range(shards_per_block)
    ]
    kv = pl.pallas_call(
        functools.partial(pack, spread_lead),
        out_shape=jax.ShapeDtypeStruct((block_count,) + piece, bf16),
        in_specs=[VMEM, VMEM],
        out_specs=VMEM,
        compiler_params=small(60),
    )(keys, values)
    kv, listed, queries = lax.optimization_barrier((kv, listed, queries))
    own = lax.all_to_all(kv, "head", 0, 0, tiled=True, axis_index_groups=spread_groups)

    table = pl.pallas_call(
        functools.partial(tables, per_span, spread_lead, ctx_lead),
        out_shape=jax.ShapeDtypeStruct((2 + slot_count, key_blocks.shape[0]), i32),
        in_specs=[SMEM, SMEM, VMEM],
        out_specs=VMEM,
        compiler_params=small(),
        cost_estimate=pl.CostEstimate(flops=2 * 10**10, bytes_accessed=2**14, transcendentals=0),
    )(me[None], span_order, listed)

    core = lax.rem(rank, 2)
    query_parts = queries.reshape(chips, 2, rows_device // group, width)
    crossing = lax.dynamic_index_in_dim(query_parts, 1 - core, 1, keepdims=False)
    sibling = lax.ppermute(crossing, "head", [(i, i ^ 1) for i in range(head_count)])
    part = jax.ShapeDtypeStruct((2, rows_device // group, width), bf16)
    bundles = pl.pallas_call(
        bundle,
        out_shape=(part,) * chips,
        in_specs=[SMEM, VMEM, VMEM],
        out_specs=(VMEM,) * chips,
        compiler_params=small(8),
    )(rank[None], query_parts.reshape(group, rows_device // group, width), sibling)

    own, table, bundles = lax.optimization_barrier((own, table, bundles))

    asked = pl.pallas_call(
        functools.partial(pick_asked, per_span, spread_lead, ctx_lead),
        out_shape=jax.ShapeDtypeStruct((ctx_count * CAP,) + piece, bf16),
        in_specs=[SMEM, SMEM, VMEM],
        out_specs=VMEM,
        compiler_params=small(),
    )(span_order, table, own)
    ctx_groups = [[i ^ ctx_lead for i in range(ctx_count)]]
    foreign = lax.all_to_all(asked, "ctx", 0, 0, tiled=True, axis_index_groups=ctx_groups)

    *bundles, _ = lax.optimization_barrier((*bundles, asked))
    arrived = [
        lax.ppermute(bundles[k], "head", [(i, i ^ (2 * k)) for i in range(head_count)])
        for k in (*range(2, chips), 1)
    ]

    kv_groups = [[g * group + (i ^ group_lead) for i in range(group)] for g in range(kv_heads)]
    foreign, arrived = lax.optimization_barrier((foreign, arrived))
    query_here = [bundles[0], arrived[-1], *arrived[:-1]]
    pairs = pl.pallas_call(
        functools.partial(pick_pairs, per_span),
        out_shape=jax.ShapeDtypeStruct((block_count * slot_count,) + piece, bf16),
        in_specs=[SMEM, SMEM, SMEM, VMEM, VMEM],
        out_specs=VMEM,
        compiler_params=small(),
    )(me[None], span_order, table, own, foreign)
    pairs = lax.all_to_all(pairs, "head", 0, 0, tiled=True, axis_index_groups=kv_groups)
    pairs = pairs.reshape((group, per_rank * slot_count) + piece)

    done = pl.pallas_call(
        functools.partial(attend, per_span, group_lead),
        out_shape=jax.ShapeDtypeStruct((group, per_rank * BLK, width), bf16),
        in_specs=[SMEM, SMEM, SMEM] + [VMEM] * (chips + 1),
        out_specs=VMEM,
        scratch_shapes=[pltpu.VMEM((per_rank, slot_count * BLK, width), bf16)] * 2,
        compiler_params=small(24),
    )(me[None], rank[None], span_order, *query_here, pairs)

    out = lax.all_to_all(done, "head", 0, 0, tiled=True, axis_index_groups=kv_groups)
    return out.reshape(rows_device, 1, width)


def solution(mesh):
    in_specs = (
        P("ctx", "head", None),
        P(("ctx", "head"), None, None),
        P(("ctx", "head"), None, None),
        P(),
        P(),
    )
    out_specs = P("ctx", "head", None)
    return jax.shard_map(body, mesh=mesh, in_specs=in_specs, out_specs=out_specs, check_vma=False)
```

```python
import functools

import jax
import jax.numpy as jnp
from jax import lax
from jax.experimental import pallas as pl
from jax.experimental.pallas import tpu as pltpu
from jax.sharding import PartitionSpec as P

BLK = 128
CAP = 2
LOG2E = 1.4426950408889634
MASKED = -1e30
SMEM = pl.BlockSpec(memory_space=pltpu.SMEM)
VMEM = pl.BlockSpec(memory_space=pltpu.VMEM)


def small(mib=4):
    return pltpu.CompilerParams(vmem_limit_bytes=mib * 2**20)


def pack(lead, key_ref, value_ref, out_ref):
    count, _, rows, width = out_ref.shape
    for i, ref in enumerate((key_ref, value_ref)):
        turned = jnp.swapaxes(ref[...].astype(jnp.float32), 0, 1).astype(jnp.bfloat16)
        turned = turned.reshape(count, rows, width)
        for j in range(count):
            out_ref[j ^ lead, i] = turned[j]


def tables(per_span, spread_lead, ctx_lead, me_ref, span_ref, listed_ref, out_ref):
    listed = listed_ref[...]
    slots, positions = listed.shape
    span_count = span_ref.shape[0]
    blocks = 2 * per_span
    me = me_ref[0]
    first = span_ref[2 * me]
    second = span_ref[2 * me + 1]
    slot = lax.broadcasted_iota(jnp.int32, listed.shape, 0)
    position = lax.broadcasted_iota(jnp.int32, listed.shape, 1)
    used = slot <= position
    span = listed // per_span
    rest = listed % per_span

    mine = used & ((span == first) | (span == second))
    block = rest + jnp.where(span == second, per_span, 0)
    low = jnp.min(jnp.where(mine, block, blocks - 1), axis=0, keepdims=True)
    high = jnp.max(jnp.where(mine, block, 0), axis=0, keepdims=True)
    low = jnp.broadcast_to(low, (8, positions))
    high = jnp.broadcast_to(high, (8, positions))
    step = 1
    while step < per_span:
        low = jnp.minimum(low, pltpu.roll(low, positions - step, 1))
        high = jnp.maximum(high, pltpu.roll(high, positions - step, 1))
        step *= 2
    out_ref[0:1, :] = low[0:1]
    out_ref[1:2, :] = high[0:1]

    at = jnp.zeros_like(listed)
    for s in range(span_count):
        at = jnp.where(span == span_ref[s], s, at)
    owner = at // 2
    held = at % 2 * per_span + rest
    asker = position // per_span
    asking = used & ((asker == first) | (asker == second))
    held_float = held.astype(jnp.float32)
    lowest = jnp.zeros(listed.shape, jnp.float32)
    for o in range(span_count // 2):
        here = owner == o
        least = jnp.where(here & asking, held_float, float(blocks))
        least = jnp.min(jnp.min(least, axis=0, keepdims=True), axis=1, keepdims=True)
        lowest = jnp.where(here, least, lowest)
    foreign = blocks + CAP * (owner ^ ctx_lead) + jnp.where(held_float > lowest, 1, 0)
    out_ref[2:2 + slots, :] = jnp.where(owner == me, held ^ spread_lead, foreign)


def pick_asked(per_span, spread_lead, ctx_lead, span_ref, table_ref, own_ref, out_ref):
    for d in range(out_ref.shape[0] // CAP):
        a = span_ref[2 * d] * per_span
        b = span_ref[2 * d + 1] * per_span
        low = jnp.minimum(table_ref[0, a], table_ref[0, b])
        high = jnp.maximum(table_ref[1, a], table_ref[1, b])
        out_ref[2 * (d ^ ctx_lead)] = own_ref[low ^ spread_lead]
        out_ref[2 * (d ^ ctx_lead) + 1] = own_ref[high ^ spread_lead]


def pick_pairs(per_span, me_ref, span_ref, table_ref, own_ref, foreign_ref, out_ref):
    own_count = own_ref.shape[0]
    slots = out_ref.shape[0] // own_count
    for block in range(own_count):
        position = span_ref[2 * me_ref[0] + block // per_span] * per_span + block % per_span
        for j in range(slots):
            at = table_ref[2 + j, position]
            mine = own_ref[jnp.minimum(at, own_count - 1)]
            theirs = foreign_ref[jnp.maximum(at - own_count, 0)]
            out_ref[block * slots + j] = jnp.where(at < own_count, mine, theirs)


def bundle(rank_ref, query_ref, sibling_ref, *out_refs):
    chip = rank_ref[0] // 2
    core = rank_ref[0] % 2
    for k, out_ref in enumerate(out_refs):
        to = chip ^ k
        out_ref[0] = query_ref[2 * to + core]
        out_ref[1] = sibling_ref[to]


def attend(per_span, lead, me_ref, rank_ref, span_ref, *refs):
    *query_refs, pair_ref, out_ref, key_all, value_all = refs
    pieces, pair_count, _, rows, width = pair_ref.shape
    blocks = key_all.shape[0]
    slots = pair_count // blocks
    factor = (width ** -0.5) * LOG2E
    chip = rank_ref[0] // 2
    core = rank_ref[0] % 2
    row = lax.broadcasted_iota(jnp.int32, (BLK, BLK), 0)
    col = lax.broadcasted_iota(jnp.int32, (BLK, BLK), 1)
    piece = (col // rows) ^ lead
    half = pieces // 2
    causal = 2 * rows * (piece % half) + rows * (piece // half) + col % rows <= row
    causal = jnp.concatenate([causal, causal], axis=0)
    for b in range(blocks):
        for j in range(slots):
            i = b * slots + j
            key_all[b, j * BLK:(j + 1) * BLK, :] = pair_ref[:, i, 0].reshape(BLK, width)
            value_all[b, j * BLK:(j + 1) * BLK, :] = pair_ref[:, i, 1].reshape(BLK, width)
    for b in range(blocks):
        block = rank_ref[0] * blocks + b
        position = span_ref[2 * me_ref[0] + block // per_span] * per_span + block % per_span
        here = slice(b * BLK, (b + 1) * BLK)
        for k, query_ref in enumerate(query_refs):
            q = query_ref[:, here, :].reshape(2 * BLK, width)
            s = lax.dot_general(
                q, key_all[b], (((1,), (1,)), ((), ())), preferred_element_type=jnp.float32
            )
            parts = [jnp.where(causal, s[:, :BLK], MASKED)]
            for j in range(1, slots):
                parts.append(jnp.where(position >= j, s[:, j * BLK:(j + 1) * BLK], MASKED))
            peak = functools.reduce(jnp.maximum, parts)
            peak = jnp.max(peak, axis=1, keepdims=True) * factor
            total = jnp.zeros((2 * BLK, BLK), jnp.float32)
            mixed = jnp.zeros((2 * BLK, width), jnp.float32)
            for j in range(slots):
                raised = jnp.exp2(parts[j] * factor - peak)
                total += raised
                mixed += jnp.dot(
                    raised.astype(jnp.bfloat16),
                    value_all[b, j * BLK:(j + 1) * BLK],
                    preferred_element_type=jnp.float32,
                )
            total = jnp.sum(total, axis=1, keepdims=True)
            result = (mixed * (1.0 / total)).astype(jnp.bfloat16)
            out_ref[2 * (chip ^ k) + core, here, :] = result[:BLK]
            out_ref[2 * (chip ^ k) + 1 - core, here, :] = result[BLK:]


def body(queries, keys, values, key_blocks, span_order):
    ctx_count = lax.axis_size("ctx")
    head_count = lax.axis_size("head")
    rows_device, _, width = queries.shape
    shard_rows, kv_heads, _ = keys.shape
    slot_count = key_blocks.shape[1]
    block_count = rows_device // BLK
    per_span = block_count // 2
    group = head_count // kv_heads
    shards_per_block = BLK // shard_rows
    halves = group // shards_per_block
    piece_rows = shard_rows // halves
    per_rank = block_count // group
    chips = group // 2
    i32 = jnp.int32
    bf16 = jnp.bfloat16
    me = lax.axis_index("ctx").astype(i32)
    spread_lead = block_count // 2 + block_count // 8
    ctx_lead = ctx_count - 2
    group_lead = 2
    rank = lax.rem(lax.axis_index("head").astype(i32), group) ^ group_lead
    piece = (2, piece_rows, width)
    listed = key_blocks.T

    spread_groups = [
        [shards_per_block * (j ^ spread_lead) + q for j in range(block_count)]
        for q in range(shards_per_block)
    ]
    kv = pl.pallas_call(
        functools.partial(pack, spread_lead),
        out_shape=jax.ShapeDtypeStruct((block_count,) + piece, bf16),
        in_specs=[VMEM, VMEM],
        out_specs=VMEM,
        compiler_params=small(60),
    )(keys, values)
    kv, listed, queries = lax.optimization_barrier((kv, listed, queries))
    own = lax.all_to_all(kv, "head", 0, 0, tiled=True, axis_index_groups=spread_groups)

    table = pl.pallas_call(
        functools.partial(tables, per_span, spread_lead, ctx_lead),
        out_shape=jax.ShapeDtypeStruct((2 + slot_count, key_blocks.shape[0]), i32),
        in_specs=[SMEM, SMEM, VMEM],
        out_specs=VMEM,
        compiler_params=small(),
        cost_estimate=pl.CostEstimate(flops=2 * 10**10, bytes_accessed=2**14, transcendentals=0),
    )(me[None], span_order, listed)

    core = lax.rem(rank, 2)
    query_parts = queries.reshape(chips, 2, rows_device // group, width)
    crossing = lax.dynamic_index_in_dim(query_parts, 1 - core, 1, keepdims=False)
    sibling = lax.ppermute(crossing, "head", [(i, i ^ 1) for i in range(head_count)])
    part = jax.ShapeDtypeStruct((2, rows_device // group, width), bf16)
    bundles = pl.pallas_call(
        bundle,
        out_shape=(part,) * chips,
        in_specs=[SMEM, VMEM, VMEM],
        out_specs=(VMEM,) * chips,
        compiler_params=small(8),
    )(rank[None], query_parts.reshape(group, rows_device // group, width), sibling)

    own, table, bundles = lax.optimization_barrier((own, table, bundles))

    asked = pl.pallas_call(
        functools.partial(pick_asked, per_span, spread_lead, ctx_lead),
        out_shape=jax.ShapeDtypeStruct((ctx_count * CAP,) + piece, bf16),
        in_specs=[SMEM, SMEM, VMEM],
        out_specs=VMEM,
        compiler_params=small(),
    )(span_order, table, own)
    ctx_groups = [[i ^ ctx_lead for i in range(ctx_count)]]
    foreign = lax.all_to_all(asked, "ctx", 0, 0, tiled=True, axis_index_groups=ctx_groups)

    *bundles, _ = lax.optimization_barrier((*bundles, asked))
    arrived = [
        lax.ppermute(bundles[k], "head", [(i, i ^ (2 * k)) for i in range(head_count)])
        for k in (*range(2, chips), 1)
    ]

    kv_groups = [[g * group + (i ^ group_lead) for i in range(group)] for g in range(kv_heads)]
    foreign, arrived = lax.optimization_barrier((foreign, arrived))
    query_here = [bundles[0], arrived[-1], *arrived[:-1]]
    pairs = pl.pallas_call(
        functools.partial(pick_pairs, per_span),
        out_shape=jax.ShapeDtypeStruct((block_count * slot_count,) + piece, bf16),
        in_specs=[SMEM, SMEM, SMEM, VMEM, VMEM],
        out_specs=VMEM,
        compiler_params=small(),
    )(me[None], span_order, table, own, foreign)
    pairs = lax.all_to_all(pairs, "head", 0, 0, tiled=True, axis_index_groups=kv_groups)
    pairs = pairs.reshape((group, per_rank * slot_count) + piece)

    done = pl.pallas_call(
        functools.partial(attend, per_span, group_lead),
        out_shape=jax.ShapeDtypeStruct((group, per_rank * BLK, width), bf16),
        in_specs=[SMEM, SMEM, SMEM] + [VMEM] * (chips + 1),
        out_specs=VMEM,
        scratch_shapes=[pltpu.VMEM((per_rank, slot_count * BLK, width), bf16)] * 2,
        compiler_params=small(24),
    )(me[None], rank[None], span_order, *query_here, pairs)

    out = lax.all_to_all(done, "head", 0, 0, tiled=True, axis_index_groups=kv_groups)
    return out.reshape(rows_device, 1, width)


def solution(mesh):
    in_specs = (
        P("ctx", "head", None),
        P(("ctx", "head"), None, None),
        P(("ctx", "head"), None, None),
        P(),
        P(),
    )
    out_specs = P("ctx", "head", None)
    return jax.shard_map(body, mesh=mesh, in_specs=in_specs, out_specs=out_specs, check_vma=False)
```

```python
import functools

import jax
import jax.numpy as jnp
from jax import lax
from jax.experimental import pallas as pl
from jax.experimental.pallas import tpu as pltpu
from jax.sharding import PartitionSpec as P

BLK = 128
CAP = 2
LOG2E = 1.4426950408889634
MASKED = -1e30
SMEM = pl.BlockSpec(memory_space=pltpu.SMEM)
VMEM = pl.BlockSpec(memory_space=pltpu.VMEM)


def small(mib=4):
    return pltpu.CompilerParams(vmem_limit_bytes=mib * 2**20)


def pack(lead, key_ref, value_ref, out_ref):
    count, _, rows, width = out_ref.shape
    for i, ref in enumerate((key_ref, value_ref)):
        turned = jnp.swapaxes(ref[...].astype(jnp.float32), 0, 1).astype(jnp.bfloat16)
        turned = turned.reshape(count, rows, width)
        for j in range(count):
            out_ref[j ^ lead, i] = turned[j]


def tables(per_span, spread_lead, ctx_lead, me_ref, span_ref, listed_ref, out_ref):
    listed = listed_ref[...]
    slots, positions = listed.shape
    span_count = span_ref.shape[0]
    blocks = 2 * per_span
    me = me_ref[0]
    first = span_ref[2 * me]
    second = span_ref[2 * me + 1]
    slot = lax.broadcasted_iota(jnp.int32, listed.shape, 0)
    position = lax.broadcasted_iota(jnp.int32, listed.shape, 1)
    used = slot <= position
    span = listed // per_span
    rest = listed % per_span

    mine = used & ((span == first) | (span == second))
    block = rest + jnp.where(span == second, per_span, 0)
    low = jnp.min(jnp.where(mine, block, blocks - 1), axis=0, keepdims=True)
    high = jnp.max(jnp.where(mine, block, 0), axis=0, keepdims=True)
    low = jnp.broadcast_to(low, (8, positions))
    high = jnp.broadcast_to(high, (8, positions))
    step = 1
    while step < per_span:
        low = jnp.minimum(low, pltpu.roll(low, positions - step, 1))
        high = jnp.maximum(high, pltpu.roll(high, positions - step, 1))
        step *= 2
    out_ref[0:1, :] = low[0:1]
    out_ref[1:2, :] = high[0:1]

    at = jnp.zeros_like(listed)
    for s in range(span_count):
        at = jnp.where(span == span_ref[s], s, at)
    owner = at // 2
    held = at % 2 * per_span + rest
    asker = position // per_span
    asking = used & ((asker == first) | (asker == second))
    held_float = held.astype(jnp.float32)
    lowest = jnp.zeros(listed.shape, jnp.float32)
    for o in range(span_count // 2):
        here = owner == o
        least = jnp.where(here & asking, held_float, float(blocks))
        least = jnp.min(jnp.min(least, axis=0, keepdims=True), axis=1, keepdims=True)
        lowest = jnp.where(here, least, lowest)
    foreign = blocks + CAP * (owner ^ ctx_lead) + jnp.where(held_float > lowest, 1, 0)
    out_ref[2:2 + slots, :] = jnp.where(owner == me, held ^ spread_lead, foreign)


def pick_asked(per_span, spread_lead, ctx_lead, span_ref, table_ref, own_ref, out_ref):
    for d in range(out_ref.shape[0] // CAP):
        a = span_ref[2 * d] * per_span
        b = span_ref[2 * d + 1] * per_span
        low = jnp.minimum(table_ref[0, a], table_ref[0, b])
        high = jnp.maximum(table_ref[1, a], table_ref[1, b])
        out_ref[2 * (d ^ ctx_lead)] = own_ref[low ^ spread_lead]
        out_ref[2 * (d ^ ctx_lead) + 1] = own_ref[high ^ spread_lead]


def pick_pairs(per_span, me_ref, span_ref, table_ref, own_ref, foreign_ref, out_ref):
    own_count = own_ref.shape[0]
    slots = out_ref.shape[0] // own_count
    for block in range(own_count):
        position = span_ref[2 * me_ref[0] + block // per_span] * per_span + block % per_span
        for j in range(slots):
            at = table_ref[2 + j, position]
            mine = own_ref[jnp.minimum(at, own_count - 1)]
            theirs = foreign_ref[jnp.maximum(at - own_count, 0)]
            out_ref[block * slots + j] = jnp.where(at < own_count, mine, theirs)


def bundle(rank_ref, query_ref, sibling_ref, *out_refs):
    chip = rank_ref[0] // 2
    core = rank_ref[0] % 2
    for k, out_ref in enumerate(out_refs):
        to = chip ^ k
        out_ref[0] = query_ref[2 * to + core]
        out_ref[1] = sibling_ref[to]


def attend(per_span, lead, me_ref, rank_ref, span_ref, *refs):
    *query_refs, pair_ref, out_ref, key_all, value_all = refs
    pieces, pair_count, _, rows, width = pair_ref.shape
    blocks = key_all.shape[0]
    slots = pair_count // blocks
    factor = (width ** -0.5) * LOG2E
    chip = rank_ref[0] // 2
    core = rank_ref[0] % 2
    row = lax.broadcasted_iota(jnp.int32, (BLK, BLK), 0)
    col = lax.broadcasted_iota(jnp.int32, (BLK, BLK), 1)
    piece = (col // rows) ^ lead
    half = pieces // 2
    key_row = 2 * rows * (piece % half) + rows * (piece // half) + col % rows
    causal = (key_row ^ rank_ref[1]) <= row
    causal = jnp.concatenate([causal, causal], axis=0)
    for b in range(blocks):
        for j in range(slots):
            i = b * slots + j
            key_all[b, j * BLK:(j + 1) * BLK, :] = pair_ref[:, i, 0].reshape(BLK, width)
            value_all[b, j * BLK:(j + 1) * BLK, :] = pair_ref[:, i, 1].reshape(BLK, width)
    for b in range(blocks):
        block = rank_ref[0] * blocks + b
        position = span_ref[2 * me_ref[0] + block // per_span] * per_span + block % per_span
        here = slice(b * BLK, (b + 1) * BLK)
        for k, query_ref in enumerate(query_refs):
            q = query_ref[:, here, :].reshape(2 * BLK, width)
            s = lax.dot_general(
                q, key_all[b], (((1,), (1,)), ((), ())), preferred_element_type=jnp.float32
            )
            parts = [jnp.where(causal, s[:, :BLK], MASKED)]
            for j in range(1, slots):
                parts.append(jnp.where(position >= j, s[:, j * BLK:(j + 1) * BLK], MASKED))
            peak = functools.reduce(jnp.maximum, parts)
            peak = jnp.max(peak, axis=1, keepdims=True) * factor
            total = jnp.zeros((2 * BLK, BLK), jnp.float32)
            mixed = jnp.zeros((2 * BLK, width), jnp.float32)
            for j in range(slots):
                raised = jnp.exp2(parts[j] * factor - peak)
                total += raised
                mixed += jnp.dot(
                    raised.astype(jnp.bfloat16),
                    value_all[b, j * BLK:(j + 1) * BLK],
                    preferred_element_type=jnp.float32,
                )
            total = jnp.sum(total, axis=1, keepdims=True)
            result = (mixed * (1.0 / total)).astype(jnp.bfloat16)
            out_ref[2 * (chip ^ k) + core, here, :] = result[:BLK]
            out_ref[2 * (chip ^ k) + 1 - core, here, :] = result[BLK:]


def body(queries, keys, values, key_blocks, span_order):
    ctx_count = lax.axis_size("ctx")
    head_count = lax.axis_size("head")
    rows_device, _, width = queries.shape
    shard_rows, kv_heads, _ = keys.shape
    slot_count = key_blocks.shape[1]
    block_count = rows_device // BLK
    per_span = block_count // 2
    group = head_count // kv_heads
    shards_per_block = BLK // shard_rows
    halves = group // shards_per_block
    piece_rows = shard_rows // halves
    per_rank = block_count // group
    chips = group // 2
    i32 = jnp.int32
    bf16 = jnp.bfloat16
    me = lax.axis_index("ctx").astype(i32)
    spread_lead = block_count // 2 + block_count // 8
    ctx_lead = ctx_count - 2
    group_lead = 2
    rank = lax.rem(lax.axis_index("head").astype(i32), group) ^ group_lead
    line = lax.div(lax.axis_index("head").astype(i32), group)
    turn = (lax.rem(line, 2) ^ lax.rem(rank, 2)) * (BLK // 2)
    ranks = jnp.stack([rank, turn])
    piece = (2, piece_rows, width)
    listed = key_blocks.T

    spread_groups = [
        [
            shards_per_block * j + (q ^ (j // halves % 2 * halves))
            for j in (i ^ spread_lead for i in range(block_count))
        ]
        for q in range(shards_per_block)
    ]
    kv = pl.pallas_call(
        functools.partial(pack, spread_lead),
        out_shape=jax.ShapeDtypeStruct((block_count,) + piece, bf16),
        in_specs=[VMEM, VMEM],
        out_specs=VMEM,
        compiler_params=small(60),
    )(keys, values)
    kv, listed, queries = lax.optimization_barrier((kv, listed, queries))
    own = lax.all_to_all(kv, "head", 0, 0, tiled=True, axis_index_groups=spread_groups)

    table = pl.pallas_call(
        functools.partial(tables, per_span, spread_lead, ctx_lead),
        out_shape=jax.ShapeDtypeStruct((2 + slot_count, key_blocks.shape[0]), i32),
        in_specs=[SMEM, SMEM, VMEM],
        out_specs=VMEM,
        compiler_params=small(),
        cost_estimate=pl.CostEstimate(flops=2 * 10**10, bytes_accessed=2**14, transcendentals=0),
    )(me[None], span_order, listed)

    core = lax.rem(rank, 2)
    query_parts = queries.reshape(chips, 2, rows_device // group, width)
    crossing = lax.dynamic_index_in_dim(query_parts, 1 - core, 1, keepdims=False)
    sibling = lax.ppermute(crossing, "head", [(i, i ^ 1) for i in range(head_count)])
    part = jax.ShapeDtypeStruct((2, rows_device // group, width), bf16)
    bundles = pl.pallas_call(
        bundle,
        out_shape=(part,) * chips,
        in_specs=[SMEM, VMEM, VMEM],
        out_specs=(VMEM,) * chips,
        compiler_params=small(8),
    )(ranks, query_parts.reshape(group, rows_device // group, width), sibling)

    own, table, bundles = lax.optimization_barrier((own, table, bundles))

    asked = pl.pallas_call(
        functools.partial(pick_asked, per_span, spread_lead, ctx_lead),
        out_shape=jax.ShapeDtypeStruct((ctx_count * CAP,) + piece, bf16),
        in_specs=[SMEM, SMEM, VMEM],
        out_specs=VMEM,
        compiler_params=small(),
    )(span_order, table, own)
    ctx_groups = [[i ^ ctx_lead for i in range(ctx_count)]]
    foreign = lax.all_to_all(asked, "ctx", 0, 0, tiled=True, axis_index_groups=ctx_groups)

    *bundles, _ = lax.optimization_barrier((*bundles, asked))
    arrived = [
        lax.ppermute(bundles[k], "head", [(i, i ^ (2 * k)) for i in range(head_count)])
        for k in (*range(2, chips), 1)
    ]

    kv_groups = [[g * group + (i ^ group_lead) for i in range(group)] for g in range(kv_heads)]
    foreign, arrived = lax.optimization_barrier((foreign, arrived))
    query_here = [bundles[0], arrived[-1], *arrived[:-1]]
    pairs = pl.pallas_call(
        functools.partial(pick_pairs, per_span),
        out_shape=jax.ShapeDtypeStruct((block_count * slot_count,) + piece, bf16),
        in_specs=[SMEM, SMEM, SMEM, VMEM, VMEM],
        out_specs=VMEM,
        compiler_params=small(),
    )(me[None], span_order, table, own, foreign)
    pairs = lax.all_to_all(pairs, "head", 0, 0, tiled=True, axis_index_groups=kv_groups)
    pairs = pairs.reshape((group, per_rank * slot_count) + piece)

    done = pl.pallas_call(
        functools.partial(attend, per_span, group_lead),
        out_shape=jax.ShapeDtypeStruct((group, per_rank * BLK, width), bf16),
        in_specs=[SMEM, SMEM, SMEM] + [VMEM] * (chips + 1),
        out_specs=VMEM,
        scratch_shapes=[pltpu.VMEM((per_rank, slot_count * BLK, width), bf16)] * 2,
        compiler_params=small(24),
    )(me[None], ranks, span_order, *query_here, pairs)

    out = lax.all_to_all(done, "head", 0, 0, tiled=True, axis_index_groups=kv_groups)
    return out.reshape(rows_device, 1, width)


def solution(mesh):
    in_specs = (
        P("ctx", "head", None),
        P(("ctx", "head"), None, None),
        P(("ctx", "head"), None, None),
        P(),
        P(),
    )
    out_specs = P("ctx", "head", None)
    return jax.shard_map(body, mesh=mesh, in_specs=in_specs, out_specs=out_specs, check_vma=False)
```

```python
import functools

import jax
import jax.numpy as jnp
from jax import lax
from jax.experimental import pallas as pl
from jax.experimental.pallas import tpu as pltpu
from jax.sharding import PartitionSpec as P

BLK = 128
CAP = 2
LOG2E = 1.4426950408889634
MASKED = -1e30
SMEM = pl.BlockSpec(memory_space=pltpu.SMEM)
VMEM = pl.BlockSpec(memory_space=pltpu.VMEM)


def small(mib=4):
    return pltpu.CompilerParams(vmem_limit_bytes=mib * 2**20)


def pack(lead, key_ref, value_ref, out_ref):
    count, _, rows, width = out_ref.shape
    for i, ref in enumerate((key_ref, value_ref)):
        turned = jnp.swapaxes(ref[...].astype(jnp.float32), 0, 1).astype(jnp.bfloat16)
        turned = turned.reshape(count, rows, width)
        for j in range(count):
            out_ref[j ^ lead, i] = turned[j]


def tables(per_span, spread_lead, ctx_lead, me_ref, span_ref, listed_ref, out_ref):
    listed = listed_ref[...]
    slots, positions = listed.shape
    span_count = span_ref.shape[0]
    blocks = 2 * per_span
    me = me_ref[0]
    first = span_ref[2 * me]
    second = span_ref[2 * me + 1]
    slot = lax.broadcasted_iota(jnp.int32, listed.shape, 0)
    position = lax.broadcasted_iota(jnp.int32, listed.shape, 1)
    used = slot <= position
    span = listed // per_span
    rest = listed % per_span

    mine = used & ((span == first) | (span == second))
    block = rest + jnp.where(span == second, per_span, 0)
    low = jnp.min(jnp.where(mine, block, blocks - 1), axis=0, keepdims=True)
    high = jnp.max(jnp.where(mine, block, 0), axis=0, keepdims=True)
    low = jnp.broadcast_to(low, (8, positions))
    high = jnp.broadcast_to(high, (8, positions))
    step = 1
    while step < per_span:
        low = jnp.minimum(low, pltpu.roll(low, positions - step, 1))
        high = jnp.maximum(high, pltpu.roll(high, positions - step, 1))
        step *= 2
    out_ref[0:1, :] = low[0:1]
    out_ref[1:2, :] = high[0:1]

    at = jnp.zeros_like(listed)
    for s in range(span_count):
        at = jnp.where(span == span_ref[s], s, at)
    owner = at // 2
    held = at % 2 * per_span + rest
    asker = position // per_span
    asking = used & ((asker == first) | (asker == second))
    held_float = held.astype(jnp.float32)
    lowest = jnp.zeros(listed.shape, jnp.float32)
    for o in range(span_count // 2):
        here = owner == o
        least = jnp.where(here & asking, held_float, float(blocks))
        least = jnp.min(jnp.min(least, axis=0, keepdims=True), axis=1, keepdims=True)
        lowest = jnp.where(here, least, lowest)
    foreign = blocks + CAP * (owner ^ ctx_lead) + jnp.where(held_float > lowest, 1, 0)
    out_ref[2:2 + slots, :] = jnp.where(owner == me, held ^ spread_lead, foreign)


def pick_asked(per_span, spread_lead, ctx_lead, span_ref, table_ref, own_ref, out_ref):
    for d in range(out_ref.shape[0] // CAP):
        a = span_ref[2 * d] * per_span
        b = span_ref[2 * d + 1] * per_span
        low = jnp.minimum(table_ref[0, a], table_ref[0, b])
        high = jnp.maximum(table_ref[1, a], table_ref[1, b])
        out_ref[2 * (d ^ ctx_lead)] = own_ref[low ^ spread_lead]
        out_ref[2 * (d ^ ctx_lead) + 1] = own_ref[high ^ spread_lead]


def pick_pairs(per_span, me_ref, span_ref, table_ref, own_ref, foreign_ref, out_ref):
    own_count = own_ref.shape[0]
    slots = out_ref.shape[0] // own_count
    for block in range(own_count):
        position = span_ref[2 * me_ref[0] + block // per_span] * per_span + block % per_span
        for j in range(slots):
            at = table_ref[2 + j, position]
            mine = own_ref[jnp.minimum(at, own_count - 1)]
            theirs = foreign_ref[jnp.maximum(at - own_count, 0)]
            out_ref[block * slots + j] = jnp.where(at < own_count, mine, theirs)


def bundle(group, lead, head_ref, query_ref, sibling_ref, *out_refs):
    rank = head_ref[0] % group ^ lead
    chip = rank // 2
    core = rank % 2
    for k, out_ref in enumerate(out_refs):
        to = chip ^ k
        out_ref[0] = query_ref[2 * to + core]
        out_ref[1] = sibling_ref[to]


def attend(per_span, group, lead, me_ref, head_ref, span_ref, *refs):
    *query_refs, pair_ref, out_ref, key_all, value_all = refs
    pieces, pair_count, _, rows, width = pair_ref.shape
    blocks = key_all.shape[0]
    slots = pair_count // blocks
    factor = (width ** -0.5) * LOG2E
    rank = head_ref[0] % group ^ lead
    chip = rank // 2
    core = rank % 2
    turn = (head_ref[0] // group % 2 ^ core) * (BLK // 2)
    row = lax.broadcasted_iota(jnp.int32, (BLK, BLK), 0)
    col = lax.broadcasted_iota(jnp.int32, (BLK, BLK), 1)
    piece = (col // rows) ^ lead
    half = pieces // 2
    key_row = 2 * rows * (piece % half) + rows * (piece // half) + col % rows
    causal = (key_row ^ turn) <= row
    causal = jnp.concatenate([causal, causal], axis=0)
    for b in range(blocks):
        for j in range(slots):
            i = b * slots + j
            key_all[b, j * BLK:(j + 1) * BLK, :] = pair_ref[:, i, 0].reshape(BLK, width)
            value_all[b, j * BLK:(j + 1) * BLK, :] = pair_ref[:, i, 1].reshape(BLK, width)
    for b in range(blocks):
        block = rank * blocks + b
        position = span_ref[2 * me_ref[0] + block // per_span] * per_span + block % per_span
        here = slice(b * BLK, (b + 1) * BLK)
        for k, query_ref in enumerate(query_refs):
            q = query_ref[:, here, :].reshape(2 * BLK, width)
            s = lax.dot_general(
                q, key_all[b], (((1,), (1,)), ((), ())), preferred_element_type=jnp.float32
            )
            parts = [jnp.where(causal, s[:, :BLK], MASKED)]
            for j in range(1, slots):
                parts.append(jnp.where(position >= j, s[:, j * BLK:(j + 1) * BLK], MASKED))
            peak = functools.reduce(jnp.maximum, parts)
            peak = jnp.max(peak, axis=1, keepdims=True)
            total = jnp.zeros((2 * BLK, BLK), jnp.float32)
            mixed = jnp.zeros((2 * BLK, width), jnp.float32)
            for j in range(slots):
                raised = jnp.exp2((parts[j] - peak) * factor)
                total += raised
                mixed += jnp.dot(
                    raised.astype(jnp.bfloat16),
                    value_all[b, j * BLK:(j + 1) * BLK],
                    preferred_element_type=jnp.float32,
                )
            total = jnp.sum(total, axis=1, keepdims=True)
            result = (mixed * (1.0 / total)).astype(jnp.bfloat16)
            out_ref[2 * (chip ^ k) + core, here, :] = result[:BLK]
            out_ref[2 * (chip ^ k) + 1 - core, here, :] = result[BLK:]


def body(queries, keys, values, key_blocks, span_order):
    ctx_count = lax.axis_size("ctx")
    head_count = lax.axis_size("head")
    rows_device, _, width = queries.shape
    shard_rows, kv_heads, _ = keys.shape
    slot_count = key_blocks.shape[1]
    block_count = rows_device // BLK
    per_span = block_count // 2
    group = head_count // kv_heads
    shards_per_block = BLK // shard_rows
    halves = group // shards_per_block
    piece_rows = shard_rows // halves
    per_rank = block_count // group
    chips = group // 2
    i32 = jnp.int32
    bf16 = jnp.bfloat16
    me = lax.axis_index("ctx").astype(i32)
    spread_lead = block_count // 2 + block_count // 8
    ctx_lead = ctx_count - 2
    group_lead = 2
    head = lax.axis_index("head").astype(i32)
    piece = (2, piece_rows, width)
    listed = key_blocks.T

    spread_groups = [
        [
            shards_per_block * j + (q ^ (j // halves % 2 * halves))
            for j in (i ^ spread_lead for i in range(block_count))
        ]
        for q in range(shards_per_block)
    ]
    kv = pl.pallas_call(
        functools.partial(pack, spread_lead),
        out_shape=jax.ShapeDtypeStruct((block_count,) + piece, bf16),
        in_specs=[VMEM, VMEM],
        out_specs=VMEM,
        compiler_params=small(60),
    )(keys, values)
    kv, listed, queries = lax.optimization_barrier((kv, listed, queries))
    own = lax.all_to_all(kv, "head", 0, 0, tiled=True, axis_index_groups=spread_groups)

    table = pl.pallas_call(
        functools.partial(tables, per_span, spread_lead, ctx_lead),
        out_shape=jax.ShapeDtypeStruct((2 + slot_count, key_blocks.shape[0]), i32),
        in_specs=[SMEM, SMEM, VMEM],
        out_specs=VMEM,
        compiler_params=small(),
        cost_estimate=pl.CostEstimate(flops=2 * 10**10, bytes_accessed=2**14, transcendentals=0),
    )(me[None], span_order, listed)

    core = lax.rem(head, 2)
    query_parts = queries.reshape(chips, 2, rows_device // group, width)
    crossing = lax.dynamic_index_in_dim(query_parts, 1 - core, 1, keepdims=False)
    sibling = lax.ppermute(crossing, "head", [(i, i ^ 1) for i in range(head_count)])
    part = jax.ShapeDtypeStruct((2, rows_device // group, width), bf16)
    bundles = pl.pallas_call(
        functools.partial(bundle, group, group_lead),
        out_shape=(part,) * chips,
        in_specs=[SMEM, VMEM, VMEM],
        out_specs=(VMEM,) * chips,
        compiler_params=small(8),
    )(head[None], query_parts.reshape(group, rows_device // group, width), sibling)

    own, table, bundles = lax.optimization_barrier((own, table, bundles))

    asked = pl.pallas_call(
        functools.partial(pick_asked, per_span, spread_lead, ctx_lead),
        out_shape=jax.ShapeDtypeStruct((ctx_count * CAP,) + piece, bf16),
        in_specs=[SMEM, SMEM, VMEM],
        out_specs=VMEM,
        compiler_params=small(),
    )(span_order, table, own)
    ctx_groups = [[i ^ ctx_lead for i in range(ctx_count)]]
    foreign = lax.all_to_all(asked, "ctx", 0, 0, tiled=True, axis_index_groups=ctx_groups)

    *bundles, _ = lax.optimization_barrier((*bundles, asked))
    arrived = [
        lax.ppermute(bundles[k], "head", [(i, i ^ (2 * k)) for i in range(head_count)])
        for k in (*range(2, chips), 1)
    ]

    kv_groups = [[g * group + (i ^ group_lead) for i in range(group)] for g in range(kv_heads)]
    foreign, arrived = lax.optimization_barrier((foreign, arrived))
    query_here = [bundles[0], arrived[-1], *arrived[:-1]]
    pairs = pl.pallas_call(
        functools.partial(pick_pairs, per_span),
        out_shape=jax.ShapeDtypeStruct((block_count * slot_count,) + piece, bf16),
        in_specs=[SMEM, SMEM, SMEM, VMEM, VMEM],
        out_specs=VMEM,
        compiler_params=small(),
    )(me[None], span_order, table, own, foreign)
    pairs = lax.all_to_all(pairs, "head", 0, 0, tiled=True, axis_index_groups=kv_groups)
    pairs = pairs.reshape((group, per_rank * slot_count) + piece)

    done = pl.pallas_call(
        functools.partial(attend, per_span, group, group_lead),
        out_shape=jax.ShapeDtypeStruct((group, per_rank * BLK, width), bf16),
        in_specs=[SMEM, SMEM, SMEM] + [VMEM] * (chips + 1),
        out_specs=VMEM,
        scratch_shapes=[pltpu.VMEM((per_rank, slot_count * BLK, width), bf16)] * 2,
        compiler_params=small(24),
    )(me[None], head[None], span_order, *query_here, pairs)

    out = lax.all_to_all(done, "head", 0, 0, tiled=True, axis_index_groups=kv_groups)
    return out.reshape(rows_device, 1, width)


def solution(mesh):
    in_specs = (
        P("ctx", "head", None),
        P(("ctx", "head"), None, None),
        P(("ctx", "head"), None, None),
        P(),
        P(),
    )
    out_specs = P("ctx", "head", None)
    return jax.shard_map(body, mesh=mesh, in_specs=in_specs, out_specs=out_specs, check_vma=False)
```

```python
import functools

import jax
import jax.numpy as jnp
from jax import lax
from jax.experimental import pallas as pl
from jax.experimental.pallas import tpu as pltpu
from jax.sharding import PartitionSpec as P

BLK = 128
CAP = 2
LOG2E = 1.4426950408889634
MASKED = -1e30
SMEM = pl.BlockSpec(memory_space=pltpu.SMEM)
VMEM = pl.BlockSpec(memory_space=pltpu.VMEM)


def small(mib=4):
    return pltpu.CompilerParams(vmem_limit_bytes=mib * 2**20)


def pack(lead, key_ref, value_ref, out_ref):
    count, _, rows, width = out_ref.shape
    for i, ref in enumerate((key_ref, value_ref)):
        turned = jnp.swapaxes(ref[...].astype(jnp.float32), 0, 1).astype(jnp.bfloat16)
        turned = turned.reshape(count, rows, width)
        for j in range(count):
            out_ref[j ^ lead, i] = turned[j]


def tables(per_span, spread_lead, ctx_lead, me_ref, span_ref, listed_ref, out_ref):
    listed = listed_ref[...]
    slots, positions = listed.shape
    span_count = span_ref.shape[0]
    blocks = 2 * per_span
    me = me_ref[0]
    first = span_ref[2 * me]
    second = span_ref[2 * me + 1]
    slot = lax.broadcasted_iota(jnp.int32, listed.shape, 0)
    position = lax.broadcasted_iota(jnp.int32, listed.shape, 1)
    used = slot <= position
    span = listed // per_span
    rest = listed % per_span

    mine = used & ((span == first) | (span == second))
    block = rest + jnp.where(span == second, per_span, 0)
    low = jnp.min(jnp.where(mine, block, blocks - 1), axis=0, keepdims=True)
    high = jnp.max(jnp.where(mine, block, 0), axis=0, keepdims=True)
    low = jnp.broadcast_to(low, (8, positions))
    high = jnp.broadcast_to(high, (8, positions))
    step = 1
    while step < per_span:
        low = jnp.minimum(low, pltpu.roll(low, positions - step, 1))
        high = jnp.maximum(high, pltpu.roll(high, positions - step, 1))
        step *= 2
    out_ref[0:1, :] = low[0:1]
    out_ref[1:2, :] = high[0:1]

    at = jnp.zeros_like(listed)
    for s in range(span_count):
        at = jnp.where(span == span_ref[s], s, at)
    owner = at // 2
    held = at % 2 * per_span + rest
    asker = position // per_span
    asking = used & ((asker == first) | (asker == second))
    held_float = held.astype(jnp.float32)
    lowest = jnp.zeros(listed.shape, jnp.float32)
    for o in range(span_count // 2):
        here = owner == o
        least = jnp.where(here & asking, held_float, float(blocks))
        least = jnp.min(jnp.min(least, axis=0, keepdims=True), axis=1, keepdims=True)
        lowest = jnp.where(here, least, lowest)
    foreign = blocks + CAP * (owner ^ ctx_lead) + jnp.where(held_float > lowest, 1, 0)
    out_ref[2:2 + slots, :] = jnp.where(owner == me, held ^ spread_lead, foreign)


def pick_asked(per_span, spread_lead, ctx_lead, span_ref, table_ref, own_ref, out_ref):
    for d in range(out_ref.shape[0] // CAP):
        a = span_ref[2 * d] * per_span
        b = span_ref[2 * d + 1] * per_span
        low = jnp.minimum(table_ref[0, a], table_ref[0, b])
        high = jnp.maximum(table_ref[1, a], table_ref[1, b])
        out_ref[2 * (d ^ ctx_lead)] = own_ref[low ^ spread_lead]
        out_ref[2 * (d ^ ctx_lead) + 1] = own_ref[high ^ spread_lead]


def pick_pairs(per_span, me_ref, span_ref, table_ref, own_ref, foreign_ref, out_ref):
    own_count = own_ref.shape[0]
    slots = out_ref.shape[0] // own_count
    for block in range(own_count):
        position = span_ref[2 * me_ref[0] + block // per_span] * per_span + block % per_span
        for j in range(slots):
            at = table_ref[2 + j, position]
            mine = own_ref[jnp.minimum(at, own_count - 1)]
            theirs = foreign_ref[jnp.maximum(at - own_count, 0)]
            out_ref[block * slots + j] = jnp.where(at < own_count, mine, theirs)


def bundle(group, lead, head_ref, query_ref, sibling_ref, *out_refs):
    rank = head_ref[0] % group ^ lead
    chip = rank // 2
    core = rank % 2
    for k, out_ref in enumerate(out_refs):
        to = chip ^ k
        out_ref[0] = query_ref[2 * to + core]
        out_ref[1] = sibling_ref[to]


def attend(per_span, group, lead, me_ref, head_ref, span_ref, *refs):
    *query_refs, pair_ref, out_ref, key_all, value_all = refs
    pieces, pair_count, _, rows, width = pair_ref.shape
    blocks = key_all.shape[0]
    slots = pair_count // blocks
    factor = (width ** -0.5) * LOG2E
    rank = head_ref[0] % group ^ lead
    chip = rank // 2
    core = rank % 2
    turn = (head_ref[0] // group % 2 ^ core) * (BLK // 2)
    row = lax.broadcasted_iota(jnp.int32, (BLK, BLK), 0)
    col = lax.broadcasted_iota(jnp.int32, (BLK, BLK), 1)
    piece = (col // rows) ^ lead
    half = pieces // 2
    key_row = 2 * rows * (piece % half) + rows * (piece // half) + col % rows
    causal = (key_row ^ turn) <= row
    causal = jnp.concatenate([causal, causal], axis=0)
    for b in range(blocks):
        for j in range(slots):
            i = b * slots + j
            key_all[b, j * BLK:(j + 1) * BLK, :] = pair_ref[:, i, 0].reshape(BLK, width)
            value_all[b, j * BLK:(j + 1) * BLK, :] = pair_ref[:, i, 1].reshape(BLK, width)
    for b in range(blocks):
        block = rank * blocks + b
        position = span_ref[2 * me_ref[0] + block // per_span] * per_span + block % per_span
        here = slice(b * BLK, (b + 1) * BLK)
        for k, query_ref in enumerate(query_refs):
            q = query_ref[:, here, :].reshape(2 * BLK, width)
            s = lax.dot_general(
                q, key_all[b], (((1,), (1,)), ((), ())), preferred_element_type=jnp.float32
            )
            parts = [jnp.where(causal, s[:, :BLK], MASKED)]
            for j in range(1, slots):
                parts.append(jnp.where(position >= j, s[:, j * BLK:(j + 1) * BLK], MASKED))
            peak = functools.reduce(jnp.maximum, parts)
            peak = jnp.max(peak, axis=1, keepdims=True)
            total = jnp.zeros((2 * BLK, BLK), jnp.float32)
            mixed = jnp.zeros((2 * BLK, width), jnp.float32)
            for j in range(slots):
                raised = jnp.exp2((parts[j] - peak) * factor)
                total += raised
                mixed += jnp.dot(
                    raised.astype(jnp.bfloat16),
                    value_all[b, j * BLK:(j + 1) * BLK],
                    preferred_element_type=jnp.float32,
                )
            total = jnp.sum(total, axis=1, keepdims=True)
            result = (mixed * (1.0 / total)).astype(jnp.bfloat16)
            out_ref[2 * (chip ^ k) + core, here, :] = result[:BLK]
            out_ref[2 * (chip ^ k) + 1 - core, here, :] = result[BLK:]


def body(queries, keys, values, key_blocks, span_order):
    ctx_count = lax.axis_size("ctx")
    head_count = lax.axis_size("head")
    rows_device, _, width = queries.shape
    shard_rows, kv_heads, _ = keys.shape
    slot_count = key_blocks.shape[1]
    block_count = rows_device // BLK
    per_span = block_count // 2
    group = head_count // kv_heads
    shards_per_block = BLK // shard_rows
    halves = group // shards_per_block
    piece_rows = shard_rows // halves
    per_rank = block_count // group
    chips = group // 2
    i32 = jnp.int32
    bf16 = jnp.bfloat16
    me = lax.axis_index("ctx").astype(i32)
    spread_lead = block_count // 2 + block_count // 8
    ctx_lead = ctx_count - 2
    group_lead = 2
    head = lax.axis_index("head").astype(i32)
    piece = (2, piece_rows, width)
    listed = key_blocks.T

    spread_groups = [
        [
            shards_per_block * j + (q ^ (j // halves % 2 * halves))
            for j in (i ^ spread_lead for i in range(block_count))
        ]
        for q in range(shards_per_block)
    ]
    kv = pl.pallas_call(
        functools.partial(pack, spread_lead),
        out_shape=jax.ShapeDtypeStruct((block_count,) + piece, bf16),
        in_specs=[VMEM, VMEM],
        out_specs=VMEM,
        compiler_params=small(60),
    )(keys, values)
    kv, listed, queries = lax.optimization_barrier((kv, listed, queries))
    own = lax.all_to_all(kv, "head", 0, 0, tiled=True, axis_index_groups=spread_groups)

    table = pl.pallas_call(
        functools.partial(tables, per_span, spread_lead, ctx_lead),
        out_shape=jax.ShapeDtypeStruct((2 + slot_count, key_blocks.shape[0]), i32),
        in_specs=[SMEM, SMEM, VMEM],
        out_specs=VMEM,
        compiler_params=small(),
        cost_estimate=pl.CostEstimate(flops=2 * 10**10, bytes_accessed=2**14, transcendentals=0),
    )(me[None], span_order, listed)

    core = lax.rem(head, 2)
    query_parts = queries.reshape(chips, 2, rows_device // group, width)
    crossing = lax.dynamic_index_in_dim(query_parts, 1 - core, 1, keepdims=False)
    sibling = lax.ppermute(crossing, "head", [(i, i ^ 1) for i in range(head_count)])
    part = jax.ShapeDtypeStruct((2, rows_device // group, width), bf16)
    bundles = pl.pallas_call(
        functools.partial(bundle, group, group_lead),
        out_shape=(part,) * chips,
        in_specs=[SMEM, VMEM, VMEM],
        out_specs=(VMEM,) * chips,
        compiler_params=small(8),
    )(head[None], query_parts.reshape(group, rows_device // group, width), sibling)

    own, table, bundles = lax.optimization_barrier((own, table, bundles))

    asked = pl.pallas_call(
        functools.partial(pick_asked, per_span, spread_lead, ctx_lead),
        out_shape=jax.ShapeDtypeStruct((ctx_count * CAP,) + piece, bf16),
        in_specs=[SMEM, SMEM, VMEM],
        out_specs=VMEM,
        compiler_params=small(),
    )(span_order, table, own)
    ctx_groups = [[i ^ ctx_lead for i in range(ctx_count)]]
    foreign = lax.all_to_all(asked, "ctx", 0, 0, tiled=True, axis_index_groups=ctx_groups)

    *bundles, _ = lax.optimization_barrier((*bundles, asked))
    arrived = [
        lax.ppermute(bundles[k], "head", [(i, i ^ (2 * k)) for i in range(head_count)])
        for k in range(chips - 1, 0, -1)
    ]

    kv_groups = [[g * group + (i ^ group_lead) for i in range(group)] for g in range(kv_heads)]
    foreign, arrived = lax.optimization_barrier((foreign, arrived))
    query_here = [bundles[0], *arrived[::-1]]
    pairs = pl.pallas_call(
        functools.partial(pick_pairs, per_span),
        out_shape=jax.ShapeDtypeStruct((block_count * slot_count,) + piece, bf16),
        in_specs=[SMEM, SMEM, SMEM, VMEM, VMEM],
        out_specs=VMEM,
        compiler_params=small(),
    )(me[None], span_order, table, own, foreign)
    pairs = lax.all_to_all(pairs, "head", 0, 0, tiled=True, axis_index_groups=kv_groups)
    pairs = pairs.reshape((group, per_rank * slot_count) + piece)

    done = pl.pallas_call(
        functools.partial(attend, per_span, group, group_lead),
        out_shape=jax.ShapeDtypeStruct((group, per_rank * BLK, width), bf16),
        in_specs=[SMEM, SMEM, SMEM] + [VMEM] * (chips + 1),
        out_specs=VMEM,
        scratch_shapes=[pltpu.VMEM((per_rank, slot_count * BLK, width), bf16)] * 2,
        compiler_params=small(24),
    )(me[None], head[None], span_order, *query_here, pairs)

    out = lax.all_to_all(done, "head", 0, 0, tiled=True, axis_index_groups=kv_groups)
    return out.reshape(rows_device, 1, width)


def solution(mesh):
    in_specs = (
        P("ctx", "head", None),
        P(("ctx", "head"), None, None),
        P(("ctx", "head"), None, None),
        P(),
        P(),
    )
    out_specs = P("ctx", "head", None)
    return jax.shard_map(body, mesh=mesh, in_specs=in_specs, out_specs=out_specs, check_vma=False)
```

```python
import functools

import jax
import jax.numpy as jnp
from jax import lax
from jax.experimental import pallas as pl
from jax.experimental.pallas import tpu as pltpu
from jax.sharding import PartitionSpec as P

BLK = 128
CAP = 2
LOG2E = 1.4426950408889634
MASKED = -1e30
SMEM = pl.BlockSpec(memory_space=pltpu.SMEM)
VMEM = pl.BlockSpec(memory_space=pltpu.VMEM)


def small(mib=4):
    return pltpu.CompilerParams(vmem_limit_bytes=mib * 2**20)


def pack(lead, key_ref, value_ref, out_ref):
    count, _, rows, width = out_ref.shape
    for i, ref in enumerate((key_ref, value_ref)):
        turned = jnp.swapaxes(ref[...].astype(jnp.float32), 0, 1).astype(jnp.bfloat16)
        turned = turned.reshape(count, rows, width)
        for j in range(count):
            out_ref[j ^ lead, i] = turned[j]


def tables(per_span, spread_lead, ctx_lead, me_ref, span_ref, listed_ref, out_ref):
    listed = listed_ref[...]
    slots, positions = listed.shape
    span_count = span_ref.shape[0]
    blocks = 2 * per_span
    me = me_ref[0]
    first = span_ref[2 * me]
    second = span_ref[2 * me + 1]
    slot = lax.broadcasted_iota(jnp.int32, listed.shape, 0)
    position = lax.broadcasted_iota(jnp.int32, listed.shape, 1)
    used = slot <= position
    span = listed // per_span
    rest = listed % per_span

    mine = used & ((span == first) | (span == second))
    block = rest + jnp.where(span == second, per_span, 0)
    low = jnp.min(jnp.where(mine, block, blocks - 1), axis=0, keepdims=True)
    high = jnp.max(jnp.where(mine, block, 0), axis=0, keepdims=True)
    low = jnp.broadcast_to(low, (8, positions))
    high = jnp.broadcast_to(high, (8, positions))
    step = 1
    while step < per_span:
        low = jnp.minimum(low, pltpu.roll(low, positions - step, 1))
        high = jnp.maximum(high, pltpu.roll(high, positions - step, 1))
        step *= 2
    out_ref[0:1, :] = low[0:1]
    out_ref[1:2, :] = high[0:1]

    at = jnp.zeros_like(listed)
    for s in range(span_count):
        at = jnp.where(span == span_ref[s], s, at)
    owner = at // 2
    held = at % 2 * per_span + rest
    asker = position // per_span
    asking = used & ((asker == first) | (asker == second))
    held_float = held.astype(jnp.float32)
    lowest = jnp.zeros(listed.shape, jnp.float32)
    for o in range(span_count // 2):
        here = owner == o
        least = jnp.where(here & asking, held_float, float(blocks))
        least = jnp.min(jnp.min(least, axis=0, keepdims=True), axis=1, keepdims=True)
        lowest = jnp.where(here, least, lowest)
    foreign = blocks + CAP * (owner ^ ctx_lead) + jnp.where(held_float > lowest, 1, 0)
    out_ref[2:2 + slots, :] = jnp.where(owner == me, held ^ spread_lead, foreign)


def pick_asked(per_span, spread_lead, ctx_lead, span_ref, table_ref, own_ref, out_ref):
    for d in range(out_ref.shape[0] // CAP):
        a = span_ref[2 * d] * per_span
        b = span_ref[2 * d + 1] * per_span
        low = jnp.minimum(table_ref[0, a], table_ref[0, b])
        high = jnp.maximum(table_ref[1, a], table_ref[1, b])
        out_ref[2 * (d ^ ctx_lead)] = own_ref[low ^ spread_lead]
        out_ref[2 * (d ^ ctx_lead) + 1] = own_ref[high ^ spread_lead]


def pick_pairs(per_span, me_ref, span_ref, table_ref, own_ref, foreign_ref, out_ref):
    own_count = own_ref.shape[0]
    slots = out_ref.shape[0] // own_count
    for block in range(own_count):
        position = span_ref[2 * me_ref[0] + block // per_span] * per_span + block % per_span
        for j in range(slots):
            at = table_ref[2 + j, position]
            mine = own_ref[jnp.minimum(at, own_count - 1)]
            theirs = foreign_ref[jnp.maximum(at - own_count, 0)]
            out_ref[block * slots + j] = jnp.where(at < own_count, mine, theirs)


def bundle(group, lead, head_ref, query_ref, sibling_ref, *out_refs):
    rank = head_ref[0] % group ^ lead
    chip = rank // 2
    core = rank % 2
    for k, out_ref in enumerate(out_refs):
        to = chip ^ k
        out_ref[0] = query_ref[2 * to + core]
        out_ref[1] = sibling_ref[to]


def attend(per_span, group, lead, me_ref, head_ref, span_ref, *refs):
    *query_refs, pair_ref, out_ref, key_all, value_all = refs
    pieces, pair_count, _, rows, width = pair_ref.shape
    blocks = key_all.shape[0]
    slots = pair_count // blocks
    factor = (width ** -0.5) * LOG2E
    rank = head_ref[0] % group ^ lead
    chip = rank // 2
    core = rank % 2
    turn = (head_ref[0] // group % 2 ^ core) * (BLK // 2)
    row = lax.broadcasted_iota(jnp.int32, (BLK, BLK), 0)
    col = lax.broadcasted_iota(jnp.int32, (BLK, BLK), 1)
    piece = (col // rows) ^ lead
    half = pieces // 2
    key_row = 2 * rows * (piece % half) + rows * (piece // half) + col % rows
    causal = (key_row ^ turn) <= row
    causal = jnp.concatenate([causal, causal], axis=0)
    for b in range(blocks):
        for j in range(slots):
            i = b * slots + j
            key_all[b, j * BLK:(j + 1) * BLK, :] = pair_ref[:, i, 0].reshape(BLK, width)
            value_all[b, j * BLK:(j + 1) * BLK, :] = pair_ref[:, i, 1].reshape(BLK, width)
    for b in range(blocks):
        block = rank * blocks + b
        position = span_ref[2 * me_ref[0] + block // per_span] * per_span + block % per_span
        here = slice(b * BLK, (b + 1) * BLK)
        for k, query_ref in enumerate(query_refs):
            q = query_ref[:, here, :].reshape(2 * BLK, width)
            s = lax.dot_general(
                q, key_all[b], (((1,), (1,)), ((), ())), preferred_element_type=jnp.float32
            )
            parts = [jnp.where(causal, s[:, :BLK], MASKED)]
            for j in range(1, slots):
                parts.append(jnp.where(position >= j, s[:, j * BLK:(j + 1) * BLK], MASKED))
            peak = functools.reduce(jnp.maximum, parts)
            peak = jnp.max(peak, axis=1, keepdims=True)
            total = jnp.zeros((2 * BLK, BLK), jnp.float32)
            mixed = jnp.zeros((2 * BLK, width), jnp.float32)
            for j in range(slots):
                raised = jnp.exp2((parts[j] - peak) * factor)
                total += raised
                mixed += jnp.dot(
                    raised.astype(jnp.bfloat16),
                    value_all[b, j * BLK:(j + 1) * BLK],
                    preferred_element_type=jnp.float32,
                )
            total = jnp.sum(total, axis=1, keepdims=True)
            result = (mixed * (1.0 / total)).astype(jnp.bfloat16)
            out_ref[2 * (chip ^ k) + core, here, :] = result[:BLK]
            out_ref[2 * (chip ^ k) + 1 - core, here, :] = result[BLK:]


def body(queries, keys, values, key_blocks, span_order):
    ctx_count = lax.axis_size("ctx")
    head_count = lax.axis_size("head")
    rows_device, _, width = queries.shape
    shard_rows, kv_heads, _ = keys.shape
    slot_count = key_blocks.shape[1]
    block_count = rows_device // BLK
    per_span = block_count // 2
    group = head_count // kv_heads
    shards_per_block = BLK // shard_rows
    halves = group // shards_per_block
    piece_rows = shard_rows // halves
    per_rank = block_count // group
    chips = group // 2
    i32 = jnp.int32
    bf16 = jnp.bfloat16
    me = lax.axis_index("ctx").astype(i32)
    spread_lead = block_count // 2 + block_count // 8
    ctx_lead = ctx_count - 3
    group_lead = 2
    head = lax.axis_index("head").astype(i32)
    piece = (2, piece_rows, width)
    listed = key_blocks.T

    spread_groups = [
        [
            shards_per_block * j + (q ^ (j // halves % 2 * halves))
            for j in (i ^ spread_lead for i in range(block_count))
        ]
        for q in range(shards_per_block)
    ]
    kv = pl.pallas_call(
        functools.partial(pack, spread_lead),
        out_shape=jax.ShapeDtypeStruct((block_count,) + piece, bf16),
        in_specs=[VMEM, VMEM],
        out_specs=VMEM,
        compiler_params=small(60),
    )(keys, values)
    kv, listed, queries = lax.optimization_barrier((kv, listed, queries))
    own = lax.all_to_all(kv, "head", 0, 0, tiled=True, axis_index_groups=spread_groups)

    table = pl.pallas_call(
        functools.partial(tables, per_span, spread_lead, ctx_lead),
        out_shape=jax.ShapeDtypeStruct((2 + slot_count, key_blocks.shape[0]), i32),
        in_specs=[SMEM, SMEM, VMEM],
        out_specs=VMEM,
        compiler_params=small(),
        cost_estimate=pl.CostEstimate(flops=2 * 10**10, bytes_accessed=2**14, transcendentals=0),
    )(me[None], span_order, listed)

    core = lax.rem(head, 2)
    query_parts = queries.reshape(chips, 2, rows_device // group, width)
    crossing = lax.dynamic_index_in_dim(query_parts, 1 - core, 1, keepdims=False)
    sibling = lax.ppermute(crossing, "head", [(i, i ^ 1) for i in range(head_count)])
    part = jax.ShapeDtypeStruct((2, rows_device // group, width), bf16)
    bundles = pl.pallas_call(
        functools.partial(bundle, group, group_lead),
        out_shape=(part,) * chips,
        in_specs=[SMEM, VMEM, VMEM],
        out_specs=(VMEM,) * chips,
        compiler_params=small(8),
    )(head[None], query_parts.reshape(group, rows_device // group, width), sibling)

    own, table, bundles = lax.optimization_barrier((own, table, bundles))

    asked = pl.pallas_call(
        functools.partial(pick_asked, per_span, spread_lead, ctx_lead),
        out_shape=jax.ShapeDtypeStruct((ctx_count * CAP,) + piece, bf16),
        in_specs=[SMEM, SMEM, VMEM],
        out_specs=VMEM,
        compiler_params=small(),
    )(span_order, table, own)
    ctx_groups = [[i ^ ctx_lead for i in range(ctx_count)]]
    foreign = lax.all_to_all(asked, "ctx", 0, 0, tiled=True, axis_index_groups=ctx_groups)

    *bundles, _ = lax.optimization_barrier((*bundles, asked))
    arrived = [
        lax.ppermute(bundles[k], "head", [(i, i ^ (2 * k)) for i in range(head_count)])
        for k in range(chips - 1, 0, -1)
    ]

    kv_groups = [[g * group + (i ^ group_lead) for i in range(group)] for g in range(kv_heads)]
    foreign, arrived = lax.optimization_barrier((foreign, arrived))
    query_here = [bundles[0], *arrived[::-1]]
    pairs = pl.pallas_call(
        functools.partial(pick_pairs, per_span),
        out_shape=jax.ShapeDtypeStruct((block_count * slot_count,) + piece, bf16),
        in_specs=[SMEM, SMEM, SMEM, VMEM, VMEM],
        out_specs=VMEM,
        compiler_params=small(),
    )(me[None], span_order, table, own, foreign)
    pairs = lax.all_to_all(pairs, "head", 0, 0, tiled=True, axis_index_groups=kv_groups)
    pairs = pairs.reshape((group, per_rank * slot_count) + piece)

    done = pl.pallas_call(
        functools.partial(attend, per_span, group, group_lead),
        out_shape=jax.ShapeDtypeStruct((group, per_rank * BLK, width), bf16),
        in_specs=[SMEM, SMEM, SMEM] + [VMEM] * (chips + 1),
        out_specs=VMEM,
        scratch_shapes=[pltpu.VMEM((per_rank, slot_count * BLK, width), bf16)] * 2,
        compiler_params=small(24),
    )(me[None], head[None], span_order, *query_here, pairs)

    out = lax.all_to_all(done, "head", 0, 0, tiled=True, axis_index_groups=kv_groups)
    return out.reshape(rows_device, 1, width)


def solution(mesh):
    in_specs = (
        P("ctx", "head", None),
        P(("ctx", "head"), None, None),
        P(("ctx", "head"), None, None),
        P(),
        P(),
    )
    out_specs = P("ctx", "head", None)
    return jax.shard_map(body, mesh=mesh, in_specs=in_specs, out_specs=out_specs, check_vma=False)
```
